32 devices in a mesh: dp: 8 (over z, y), nbr: 4 (over x, core).
Axes of the slice: x: 2, y: 2, z: 4, core: 2. Of those that a mesh axis runs over, the one named last changes fastest.
Arguments:
- queries: bfloat16 [6144, 4096], P(('dp', 'nbr')), may hold values from -256 to 256
- cotangent: bfloat16 [6144, 4096], P(('dp', 'nbr')), may hold values from -1 to 1
- pool: bfloat16 [64, 128, 896], P('dp', 'nbr'), may hold values from -60 to 60
- enc_gain: float32 [896], replicated, may hold values from 0.25 to 1.75
- enc_weight: bfloat16 [896, 896], replicated, may hold values from -0.1875 to 0.1875
- k_weight: bfloat16 [896, 4096], P(None, 'nbr'), may hold values from -0.1875 to 0.1875
- v_weight: bfloat16 [896, 4096], P(None, 'nbr'), may hold values from -0.1875 to 0.1875
- nbr_owner: int32 [96, 1], replicated, may hold values from 0 to 7; in each aligned block of 12 rows (0 to 11, 12 to 23, ...) at most 2 rows name the same one
- nbr_slot: int32 [96, 1], replicated, may hold values from 0 to 7
Outputs:
- attended: bfloat16 [6144, 4096], P(('dp', 'nbr'))
- grad_k: float32 [896, 4096], P('dp', 'nbr')
- grad_v: float32 [896, 4096], P('dp', 'nbr')
The draws below stay inside these ranges and needn't reach their ends.
Inputs may be any that keep to these rules, and one draw needn't show every extreme that they name: `nbr_owner`: within the 12 groups of one sequence at most 2 name the same index of dp, and this bound is reached.
All inputs are finite; a program needn't handle non-finite values.
Results may differ from the reference program's by a relative error of at most 0.035.
The reference program's roundings to bfloat16 on the way (of `normed`, `encoded`, `neighbours` and `weights`) count: a program that leaves them out, or rounds other values in their place, can miss the bound.
Values may be sent and summed in bfloat16 or wider, within the bound.
A program may use at most 128 MiB of HBM per device.

```python
import math
import jax
import jax.numpy as jnp
import numpy as np
from jax import lax

D = 4096
HEADS = 32
HEAD = 128
E = 896
GROUP = 64
RL = 128
KN = 1
CAP = 2
NB = 8
LEN = 768
CH_ROW = 12
TOKENS = 6144
GROUPS = 96
POOL = 64
N_DP = 8


def draw_queries(key, part):
    base_key = jax.random.fold_in(key, 0)
    base = jnp.clip(jax.random.normal(base_key, (TOKENS, D), jnp.float32), -6.0, 6.0)
    return base.astype(jnp.bfloat16)


def draw_pool(key, part):
    base_key, row_key, col_key = jax.random.split(key, 3)
    base = jnp.clip(jax.random.normal(base_key, (POOL, RL, E), jnp.float32), -6.0, 6.0)
    lower, upper = (0.1, 1.0)
    row_scale = jnp.exp(jax.random.uniform(row_key, (POOL, RL, 1), jnp.float32, math.log(lower), math.log(upper)))
    col_scale = jnp.exp(jax.random.uniform(col_key, (1, 1, E), jnp.float32, math.log(lower), math.log(upper)))
    return (base * row_scale * col_scale).astype(jnp.bfloat16)


def with_ends(drawn, own_key, smallest, largest):
    longest = drawn.shape.index(max(drawn.shape))
    spots = []
    for shift in (0, 1):
        where = [jax.random.randint(jax.random.fold_in(own_key, axis), (), 0, length) for axis, length in enumerate(drawn.shape)]
        where[longest] = (where[longest] + shift) % drawn.shape[longest]
        spots.append(tuple(where))
    return drawn.at[spots[0]].set(smallest).at[spots[1]].set(largest)


def shard_levels(own_key, dims, shards, low, top_value):
    loudness = 1.0
    for dim, parts in shards:
        draws = jax.random.uniform(jax.random.fold_in(jax.random.fold_in(own_key, 6), dim), (parts,), jnp.float32, low / len(shards), top_value / len(shards))
        loudness = loudness * jnp.repeat(jnp.exp(draws), dims[dim] // parts).reshape((-1,) + (1,) * (len(dims) - 1 - dim))
    return loudness


def shared_out(key, own, number, rows, count, top, limit, slope):
    order = jax.random.permutation(key, count)
    crowded, ordinary = portions_of(count, rows * top, limit, slope, True), portions_of(count, rows * top, limit, slope, False)
    places = jnp.arange(count)

    def named(tallies, turn):
        used = int((tallies > 0).sum())
        fixed = max(1, used // 4)
        moved = fixed + (places - fixed + turn * (used - fixed)) % max(1, count - fixed)
        return jnp.zeros((count,), jnp.int32).at[order[jnp.where(places < fixed, places, moved)]].set(jnp.asarray(tallies, jnp.int32))

    tallies = jnp.where(number % 4 == 0, named(crowded, number // 4), named(ordinary, number - number // 4 - 1))
    mixed = jax.random.permutation(jax.random.fold_in(own, 3), count)
    donor, receiver = mixed[0:count // 2 * 2:2], mixed[1:count // 2 * 2:2]
    margin = jnp.minimum(tallies[donor] - 1, limit - tallies[receiver]) // 2
    margin = jnp.where((donor == order[0]) | (receiver == order[0]) | (tallies[receiver] == 0), 0, jnp.maximum(margin, 0))
    moved = jax.random.randint(jax.random.fold_in(own, 4), (count // 2,), 0, 1 << 20) % (margin + 1)
    tallies = tallies.at[donor].add(-moved).at[receiver].add(moved)
    items = jnp.searchsorted(jnp.cumsum(tallies), jnp.arange(rows * top), side="right").astype(jnp.int32)
    grid = items.reshape(top, rows).T
    grid = grid[jax.random.permutation(jax.random.fold_in(own, 1), rows)]
    turn = jax.random.randint(jax.random.fold_in(own, 2), (rows, 1), 0, top)
    return jnp.take_along_axis(grid, (jnp.arange(top)[None, :] + turn) % top, axis=1)


def portions_of(count, total, limit, slope, full):
    portions = [(1 << 20) // math.isqrt(grade ** slope) + 1 for grade in range(1, count + 1)]
    largest = limit if full else min(limit, max(-(-total // count), total * portions[0] // sum(portions)))
    least = 1 if total - largest >= count - 1 else 0
    holding, surplus = [largest] + [least] * (count - 1), total - largest - least * (count - 1)
    while surplus > 0:
        movable = [i for i in range(1, count) if holding[i] < largest] or [i for i in range(1, count) if holding[i] < limit]
        whole, budget = sum([portions[i] for i in movable]), surplus
        for i in movable:
            addition = min(limit - holding[i], max(1, budget * portions[i] // whole), surplus)
            holding[i] = holding[i] + addition
            surplus = surplus - addition
    return np.array(holding)


def normal_values(key, extent, scale, limit, shards=(), kind=jnp.bfloat16):
    drawn = jax.random.normal(key, extent, jnp.float32) * scale
    if len(shards) > 0:
        drawn = shard_levels(key, extent, shards, -0.22, 0.18) * drawn
    return jnp.clip(drawn, min=-limit, max=limit).astype(kind)


def setup_inputs(seed: int = 0) -> dict:
    arg_keys = jax.random.split(jax.random.key(seed), 10)
    queries = draw_queries(jax.random.fold_in(arg_keys[9], 71), 0)
    cotangent = normal_values(arg_keys[1], (TOKENS, D), 0.0625, 1.0, ((0, 32),))
    pool = draw_pool(jax.random.fold_in(arg_keys[9], 71), 0)
    enc_gain = jnp.clip(1.0 + 0.15 * jax.random.normal(arg_keys[3], (E,), jnp.float32), 0.25, 1.75)
    enc_weight = normal_values(arg_keys[4], (E, E), E ** -0.5, 0.1875)
    k_weight = normal_values(arg_keys[5], (E, D), E ** -0.5, 0.1875, ((1, 4),))
    v_weight = normal_values(arg_keys[6], (E, D), E ** -0.5, 0.1875, ((1, 4),))
    nbr_owner_keys = jax.random.split(jax.random.fold_in(arg_keys[7], 1), GROUPS // CH_ROW)
    nbr_owner_turns = jax.random.permutation(jax.random.fold_in(arg_keys[7], 3), GROUPS // CH_ROW)
    nbr_owner = jax.vmap(lambda own, number: shared_out(jax.random.fold_in(arg_keys[7], 2), own, number, CH_ROW, N_DP, KN, CAP, 2))(nbr_owner_keys, nbr_owner_turns).reshape((GROUPS, KN))
    nbr_slot = with_ends(jax.random.randint(arg_keys[8], (GROUPS, KN), 0, NB), jax.random.fold_in(arg_keys[8], 1), 0, NB - 1).astype(jnp.int32)
    return {"queries": queries, "cotangent": cotangent, "pool": pool, "enc_gain": enc_gain, "enc_weight": enc_weight, "k_weight": k_weight, "v_weight": v_weight, "nbr_owner": nbr_owner, "nbr_slot": nbr_slot}


def encode(blocks, gain_vec, weight):
    widened = blocks.astype(jnp.float32)
    mean_sq = lax.optimization_barrier(jnp.mean(widened * widened, axis=-1, keepdims=True))
    normed = (widened * lax.rsqrt(mean_sq + 1e-06) * gain_vec).astype(jnp.bfloat16)
    feature_width = blocks.shape[-1]
    combined = jnp.dot(normed.reshape(-1, feature_width), weight, preferred_element_type=jnp.float32)
    return (widened + jax.nn.gelu(combined.reshape(widened.shape))).astype(jnp.bfloat16)

def attend(q_heads, key_rows, value_rows, group_len):
    offset_rows = group_len - 1
    seq_len, head_count, head_size = q_heads.shape
    blank_rows = jnp.zeros((offset_rows, head_count, head_size), q_heads.dtype)
    shifted = jnp.concatenate([q_heads[offset_rows:], blank_rows], axis=0)
    shifted = shifted.reshape(-1, group_len, head_count, head_size)
    scores = jnp.einsum('cqhd,ckhd->chqk', shifted.astype(jnp.float32), key_rows.astype(jnp.float32))
    scores = scores * head_size ** (-0.5)
    weights = jax.nn.softmax(scores, axis=-1).astype(jnp.bfloat16)
    combined = jnp.einsum('chqk,ckhd->cqhd', weights.astype(jnp.float32), value_rows.astype(jnp.float32))
    combined = combined.astype(jnp.bfloat16).reshape(seq_len, head_count, head_size)
    return jnp.concatenate([blank_rows, combined[:seq_len - offset_rows]], axis=0)

def reference(queries, cotangent, pool, enc_gain, enc_weight, k_weight, v_weight, nbr_owner, nbr_slot):
    encoded = encode(pool, enc_gain, enc_weight)
    block_ids = (nbr_owner * NB + nbr_slot)[:, 0].astype(jnp.int32)

    def sequence_step(totals, seq_index):
        first_row = seq_index * LEN
        q_rows = lax.dynamic_slice_in_dim(queries, first_row, LEN, 0)
        g_rows = lax.dynamic_slice_in_dim(cotangent, first_row, LEN, 0)
        chosen = lax.dynamic_slice_in_dim(block_ids, seq_index * CH_ROW, CH_ROW, 0)
        neighbours = jnp.take(encoded, chosen, axis=0)
        flat_enc = neighbours.reshape(CH_ROW * RL, E)
        key_rows = jnp.dot(flat_enc, k_weight, preferred_element_type=jnp.float32).astype(jnp.bfloat16)
        value_rows = jnp.dot(flat_enc, v_weight, preferred_element_type=jnp.float32).astype(jnp.bfloat16)
        q_heads = q_rows.reshape(LEN, HEADS, HEAD)

        def attend_here(keys_in, values_in):
            shaped_keys = keys_in.reshape(CH_ROW, RL, HEADS, HEAD)
            shaped_values = values_in.reshape(CH_ROW, RL, HEADS, HEAD)
            return attend(q_heads, shaped_keys, shaped_values, GROUP).reshape(LEN, D)
        attended, pullback = jax.vjp(attend_here, key_rows, value_rows)
        key_grads, value_grads = pullback(g_rows)
        grad_key = jnp.dot(flat_enc.T, key_grads, preferred_element_type=jnp.float32)
        grad_value = jnp.dot(flat_enc.T, value_grads, preferred_element_type=jnp.float32)
        return ((totals[0] + grad_key, totals[1] + grad_value), attended)
    blank_grad = jnp.zeros((E, D), jnp.float32)
    totals, attended_all = lax.scan(sequence_step, (blank_grad, blank_grad), jnp.arange(N_DP).astype(jnp.int32))
    return (attended_all.reshape(TOKENS, D), totals[0], totals[1])
```

```python
import jax
import jax.numpy as jnp
from jax import lax
from jax.experimental import pallas as pl
from jax.experimental.pallas import tpu as pltpu
from jax.sharding import PartitionSpec as P

HEAD = 128
GROUP = 64
CAP = 2
BF = jnp.bfloat16
F32 = jnp.float32


def encode(blocks, gain_vec, weight):
    widened = blocks.astype(F32)
    mean_sq = jnp.mean(widened * widened, axis=-1, keepdims=True)
    normed = (widened * lax.rsqrt(mean_sq + 1e-06) * gain_vec).astype(BF)
    combined = jnp.dot(normed, weight, preferred_element_type=F32)
    return (widened + jax.nn.gelu(combined)).astype(BF)


def pick_rows(chosen, rows, tokens):
    m, n = chosen.shape
    eye = jnp.eye(tokens, dtype=BF)
    full = chosen.astype(BF)[:, None, :, None] * eye[None, :, None, :]
    full = full.reshape(m * tokens, n * tokens)
    return jnp.dot(full, rows, preferred_element_type=F32).astype(BF)


def attention_body(q_ref, g_ref, k_ref, v_ref, o_ref, dk_ref, dv_ref):
    heads = q_ref.shape[1] // HEAD
    parts, _, tokens, _ = k_ref.shape
    keys = parts * tokens
    scale = HEAD ** (-0.5)
    over_last = (((1,), (1,)), ((), ()))
    over_first = (((0,), (0,)), ((), ()))
    for first in range(0, heads, 4):
        held = []
        for h in range(first, min(first + 4, heads)):
            cols = slice(h * HEAD, (h + 1) * HEAD)
            k = k_ref[:, 0, :, cols].reshape(keys, HEAD)
            v = v_ref[:, 0, :, cols].reshape(keys, HEAD)
            s = lax.dot_general(q_ref[:, cols], k, over_last, preferred_element_type=F32)
            dw = lax.dot_general(g_ref[:, cols], v, over_last, preferred_element_type=F32)
            held.append((cols, v, s * scale, dw.astype(BF).astype(F32)))
        ready = []
        for cols, v, s, dw in held:
            e = jnp.exp(s - jnp.max(s, axis=-1, keepdims=True))
            p = e * (1.0 / jnp.sum(e, axis=-1, keepdims=True))
            ds = p * (dw - jnp.sum(dw * p, axis=-1, keepdims=True)) * scale
            ready.append((cols, v, p.astype(BF), ds.astype(BF)))
        for cols, v, w, ds in ready:
            q, g = q_ref[:, cols], g_ref[:, cols]
            o_ref[:, cols] = jnp.dot(w, v, preferred_element_type=F32).astype(BF)
            dk = lax.dot_general(ds, q, over_first, preferred_element_type=F32)
            dv = lax.dot_general(w, g, over_first, preferred_element_type=F32)
            dk_ref[:, 0, :, cols] = dk.astype(BF).reshape(parts, tokens, HEAD)
            dv_ref[:, 0, :, cols] = dv.astype(BF).reshape(parts, tokens, HEAD)


def attention(q, g, k, v):
    length, width = q.shape
    parts, groups, tokens, _ = k.shape
    row = pl.BlockSpec((GROUP, width), lambda c: (c, 0))
    block = pl.BlockSpec((parts, 1, tokens, width), lambda c: (0, c, 0, 0))
    work = 10 * length * parts * tokens * width
    return pl.pallas_call(
        attention_body,
        grid=(groups,),
        in_specs=[row, row, block, block],
        out_specs=[row, block, block],
        out_shape=[
            jax.ShapeDtypeStruct(q.shape, BF),
            jax.ShapeDtypeStruct(k.shape, BF),
            jax.ShapeDtypeStruct(v.shape, BF),
        ],
        compiler_params=pltpu.CompilerParams(vmem_limit_bytes=32 * 2**20),
        cost_estimate=pl.CostEstimate(
            flops=work,
            bytes_accessed=6 * length * width + 8 * k.size,
            transcendentals=length * parts * tokens * width // HEAD,
        ),
    )(q, g, k, v)


def exchange(x, axis, split, join):
    n = lax.axis_size(axis)
    me = lax.axis_index(axis)
    span = x.shape[split] // n
    step = x.shape[join]
    parts = []
    for d in range(n):
        piece = lax.dynamic_slice_in_dim(x, (me ^ d) * span, span, split)
        if d:
            piece = lax.ppermute(piece, axis, [(i, i ^ d) for i in range(n)])
        parts.append(piece)
    shape = list(parts[0].shape)
    shape[join] = n * step
    whole = jnp.zeros(shape, x.dtype)
    for d, piece in enumerate(parts):
        whole = lax.dynamic_update_slice_in_dim(whole, piece, (me ^ d) * step, join)
    return whole


def halving(total, axis, turn):
    n = lax.axis_size(axis)
    me = lax.axis_index(axis)
    count = n.bit_length() - 1
    bits = [(i + turn) % count for i in range(count)]
    rows, width = total.shape
    current = total.reshape((2,) * count + (rows // n, width))
    left = list(range(count - 1, -1, -1))
    for bit in bits:
        place = left.index(bit)
        left.pop(place)
        mine = (me >> bit) & 1
        away = lax.dynamic_index_in_dim(current, 1 - mine, place, keepdims=False)
        keep = lax.dynamic_index_in_dim(current, mine, place, keepdims=False)
        pairs = [(i, i ^ (1 << bit)) for i in range(n)]
        current = keep + lax.ppermute(away.astype(BF), axis, pairs).astype(F32)
    return current


def staged(
    queries, cotangent, pool, enc_gain, enc_weight, k_weight, v_weight, nbr_owner, nbr_slot
):
    dp_count = lax.axis_size("dp")
    nbr_count = lax.axis_size("nbr")
    me = lax.axis_index("dp")
    held, tokens, enc_width = pool.shape
    per_row = nbr_owner.shape[0] // dp_count

    owners = nbr_owner[:, 0].reshape(dp_count, per_row)
    slots = nbr_slot[:, 0].reshape(dp_count, per_row)
    same = owners[:, :, None] == owners[:, None, :]
    earlier = jnp.tril(jnp.ones((per_row, per_row), jnp.bool_), -1)
    rank = jnp.sum((same & earlier[None]).astype(jnp.int32), axis=-1)

    ranks = jnp.arange(CAP, dtype=jnp.int32)
    blocks = jnp.arange(held, dtype=jnp.int32)
    mine = (owners == me)[:, None, :] & (rank[:, None, :] == ranks[None, :, None])
    send = jnp.any(
        mine[:, :, None, :] & (slots[:, None, None, :] == blocks[None, None, :, None]), axis=-1
    ).reshape(dp_count * CAP, held)
    enc = encode(pool.reshape(held * tokens, enc_width), enc_gain, enc_weight)
    outgoing = pick_rows(send, enc, tokens)
    arrived = lax.all_to_all(outgoing, "dp", split_axis=0, concat_axis=0, tiled=True)

    q_rows = exchange(queries, "nbr", 1, 0)
    arrived, q_rows = lax.optimization_barrier((arrived, q_rows))

    place = lax.dynamic_slice_in_dim(owners * CAP + rank, me, 1, 0)[0]
    take = place[:, None] == jnp.arange(dp_count * CAP, dtype=jnp.int32)[None, :]
    picked = pick_rows(take, arrived, tokens)
    flat_enc = lax.all_gather(picked, "nbr", axis=0, tiled=True)

    g_rows = exchange(cotangent, "nbr", 1, 0)
    seq_len, width = q_rows.shape
    lead = GROUP - 1
    blank = jnp.zeros((lead, width), BF)
    q_rows = jnp.concatenate([q_rows[lead:], blank], axis=0)
    g_rows = jnp.concatenate([g_rows[lead:], blank], axis=0)

    shape4 = (nbr_count, per_row, tokens, width)
    keys = jnp.dot(flat_enc, k_weight, preferred_element_type=F32).astype(BF)
    values = jnp.dot(flat_enc, v_weight, preferred_element_type=F32).astype(BF)
    out, dk, dv = attention(q_rows, g_rows, keys.reshape(shape4), values.reshape(shape4))

    over_first = (((0,), (0,)), ((), ()))

    def weight_grad(grads):
        return lax.dot_general(
            flat_enc, grads.reshape(-1, width), over_first, preferred_element_type=F32
        )

    grad_v = halving(weight_grad(dv), "dp", 0)
    product_k = weight_grad(dk)
    cut = width // HEAD * 3 // 8 * HEAD
    grad_k = jnp.concatenate(
        [halving(product_k[:, :cut], "dp", 0), halving(product_k[:, cut:], "dp", 1)], axis=1
    )
    out = jnp.concatenate([blank, out[: seq_len - lead]], axis=0)
    merged = exchange(out, "nbr", 0, 1)
    return (merged, grad_k, grad_v)


MESH = pl.DeviceIdType.MESH
ROWS = 16
PAIR = 2 * HEAD
LAST = (((1,), (1,)), ((), ()))
FIRST = (((0,), (0,)), ((), ()))


def gelu(x):
    return jax.nn.gelu(x)


def fused_body(
    code_ref, gain_ref, q_hbm, g_hbm, pool_hbm, encw_hbm, wk_hbm, wv_hbm,
    att_hbm, gk_ref, gv_ref,
    pool_v, encw_v, w_v, local, outbox, inboxes, enc, enc_t, qs, gs, os,
    kv, dkv, dw, part_a, send_a, land_a, part_b, send_b, land_b,
    load_sem, qg_send, qg_recv, qg_own, a2a_send, a2a_recv, gat_send, gat_recv,
    att_send, att_recv, att_own, ra_send, ra_recv, rb_send, rb_recv,
):
    n_dp, n_nbr = lax.axis_size("dp"), lax.axis_size("nbr")
    dp, nbr = lax.axis_index("dp"), lax.axis_index("nbr")
    halves, held, _, width = local.shape
    groups = enc.shape[1]
    pairs, _, _ = qs.shape
    own_rows = q_hbm.shape[0]
    keys = groups * n_nbr * ROWS
    per_group = n_nbr * ROWS
    bits = n_dp.bit_length() - 1

    chip, core = nbr // 2, nbr % 2
    mate = chip * 2 + (1 - core)
    across = ((chip + 1) * 2) % n_nbr + core
    diagonal = ((chip + 1) * 2) % n_nbr + (1 - core)
    nbr_peers = (across, diagonal, mate)
    dp_peers = [(dp + k) % n_dp for k in range(1, n_dp)]

    loads = [
        pltpu.make_async_copy(pool_hbm, pool_v, load_sem.at[0]),
        pltpu.make_async_copy(encw_hbm, encw_v, load_sem.at[1]),
        pltpu.make_async_copy(wk_hbm, w_v.at[0], load_sem.at[2]),
        pltpu.make_async_copy(wv_hbm, w_v.at[1], load_sem.at[3]),
    ]
    loads[0].start()
    loads[1].start()

    barrier = pltpu.get_barrier_semaphore()
    for peer in nbr_peers:
        pl.semaphore_signal(barrier, inc=1, device_id=(dp, peer), device_id_type=MESH)
    for peer in dp_peers:
        pl.semaphore_signal(barrier, inc=1, device_id=(peer, nbr), device_id_type=MESH)
    pl.semaphore_wait(barrier, len(nbr_peers) + len(dp_peers))

    own_at = pl.ds(pl.multiple_of(nbr * own_rows, own_rows), own_rows)

    def head_cols(peer, p):
        return pl.ds(pl.multiple_of((peer * pairs + p) * PAIR, PAIR), PAIR)

    def qg_copies(p):
        made = []
        for t, (src, dst) in enumerate(((q_hbm, qs), (g_hbm, gs))):
            for k, peer in enumerate(nbr_peers):
                made.append(
                    pltpu.make_async_remote_copy(
                        src_ref=src.at[:, head_cols(peer, p)],
                        dst_ref=dst.at[p, own_at, :],
                        send_sem=qg_send.at[p, t, k],
                        recv_sem=qg_recv.at[p, t, k],
                        device_id=(dp, peer),
                        device_id_type=MESH,
                    )
                )
        return made

    def qg_local(p):
        return [
            pltpu.make_async_copy(
                src.at[:, head_cols(nbr, p)], dst.at[p, own_at, :], qg_own.at[p, t]
            )
            for t, (src, dst) in enumerate(((q_hbm, qs), (g_hbm, gs)))
        ]

    def start(copies):
        for c in copies:
            c.start()

    for p in range(QG_FIRST):
        start(qg_copies(p))
    loads[2].start()
    loads[3].start()
    for p in range(pairs):
        start(qg_local(p))

    me = dp

    def chosen_for(s):
        count = jnp.int32(0)
        picks = [jnp.int32(0)] * CAP
        for u in range(groups):
            code = code_ref[s * groups + u]
            hit = code // held == me
            for r in range(CAP):
                picks[r] = jnp.where(hit & (count == r), code % held, picks[r])
            count = count + jnp.where(hit, 1, 0)
        return picks

    chosen = [chosen_for(s) for s in range(n_dp)]
    owners = [code_ref[me * groups + u] // held for u in range(groups)]
    places = []
    for u in range(groups):
        rank = jnp.int32(0)
        for w in range(u):
            rank = rank + jnp.where(owners[w] == owners[u], 1, 0)
        places.append(owners[u] * CAP + rank)

    def a2a_copies(h):
        return [
            pltpu.make_async_remote_copy(
                src_ref=outbox.at[h, peer],
                dst_ref=inboxes[h].at[pl.ds(pl.multiple_of(me * CAP, CAP), CAP)],
                send_sem=a2a_send.at[h, k],
                recv_sem=a2a_recv.at[h, k],
                device_id=(peer, nbr),
                device_id_type=MESH,
            )
            for k, peer in enumerate(dp_peers)
        ]

    loads[0].wait()
    loads[1].wait()
    for h in range(halves):
        x = pool_v[:, h * ROWS : (h + 1) * ROWS, :].reshape(held * ROWS, width).astype(F32)
        mean_sq = jnp.mean(x * x, axis=-1, keepdims=True)
        normed = (x * lax.rsqrt(mean_sq + 1e-06) * gain_ref[...]).astype(BF)
        combined = jnp.dot(normed, encw_v[...], preferred_element_type=F32)
        local[h] = (x + gelu(combined)).astype(BF).reshape(held, ROWS, width)
        for s in range(n_dp):
            for r in range(CAP):
                outbox[h, s, r] = local[h, chosen[s][r]]
        start(a2a_copies(h))
        for r in range(CAP):
            inboxes[h][me * CAP + r] = outbox[h, me, r]

    tail = jnp.zeros((GROUP, PAIR), BF)
    for p in range(pairs):
        qs[p, groups * GROUP : (groups + 1) * GROUP, :] = tail
        gs[p, groups * GROUP : (groups + 1) * GROUP, :] = tail
        os[p, 0:GROUP, :] = tail

    def spread(h):
        part = enc.at[h, :, nbr]
        return [
            pltpu.make_async_remote_copy(
                src_ref=part, dst_ref=part,
                send_sem=gat_send.at[h, k], recv_sem=gat_recv.at[h, k],
                device_id=(dp, peer), device_id_type=MESH,
            )
            for k, peer in enumerate((across, mate))
        ]

    def forward(h):
        part = enc.at[h, :, across]
        return pltpu.make_async_remote_copy(
            src_ref=part, dst_ref=part,
            send_sem=gat_send.at[h, 2], recv_sem=gat_recv.at[h, 2],
            device_id=(dp, mate), device_id_type=MESH,
        )

    def transpose(h):
        step = HEAD // per_group
        for u in range(0, groups, step):
            at = h * groups * per_group + u * per_group
            block = enc[h, u : u + step].reshape(HEAD, width)
            enc_t[:, at : at + HEAD] = block.T

    for h in range(halves):
        for c in a2a_copies(h):
            c.wait_recv()
        for u in range(groups):
            enc[h, u, nbr] = inboxes[h][places[u]]
        start(spread(h))
        if QG_FIRST + h < pairs:
            start(qg_copies(QG_FIRST + h))
    for h in range(halves):
        spread(h)[0].wait_recv()
        forward(h).start()
        spread(h)[1].wait_recv()
        forward(h).wait_recv()
        transpose(h)
    for p in range(QG_FIRST + halves, pairs):
        start(qg_copies(p))
    loads[2].wait()
    loads[3].wait()

    def project(p):
        cols = slice(p * PAIR, (p + 1) * PAIR)
        for h in range(halves):
            def tile(i, _):
                u = i * TILE_GROUPS
                rows = TILE_GROUPS * per_group
                e = enc[h, pl.ds(u, TILE_GROUPS)].reshape(rows, width)
                at = pl.ds(pl.multiple_of(h * groups * per_group + u * per_group, rows), rows)
                for t in range(2):
                    kv[t, at, :] = jnp.dot(
                        e, w_v[t, :, cols], preferred_element_type=F32
                    ).astype(BF)
                return 0
            lax.fori_loop(0, groups // TILE_GROUPS, tile, 0)

    scale = HEAD ** (-0.5)
    last_row = lax.broadcasted_iota(jnp.int32, (ROWS, PAIR), 0) == ROWS - 1
    blank = jnp.zeros((GROUP, HEAD), BF)

    def rows_of(ref, p, u):
        here = ref[p, pl.ds(pl.multiple_of(u * GROUP + GROUP - ROWS, ROWS), ROWS), :]
        after = ref[p, pl.ds(pl.multiple_of((u + 1) * GROUP, GROUP), GROUP), :]
        end = jnp.where(last_row, here, after[GROUP - ROWS :])
        got = jnp.concatenate([after[: GROUP - ROWS], end], axis=0)
        return jnp.concatenate(
            [
                jnp.concatenate([got[:, :HEAD], blank], axis=1),
                jnp.concatenate([blank, got[:, HEAD:]], axis=1),
            ],
            axis=0,
        )

    def key_rows(u):
        return [
            pl.ds(pl.multiple_of(h * groups * per_group + u * per_group, per_group), per_group)
            for h in range(halves)
        ]

    def attend(p):
        def several(i, _):
            us = [i * TOGETHER + j for j in range(TOGETHER)]
            held_now = []
            for u in us:
                at = key_rows(u)
                k = jnp.concatenate([kv[0, a, :] for a in at], axis=0)
                v = jnp.concatenate([kv[1, a, :] for a in at], axis=0)
                q, g = rows_of(qs, p, u), rows_of(gs, p, u)
                s = lax.dot_general(k, q, LAST, preferred_element_type=F32) * scale
                d = lax.dot_general(v, g, LAST, preferred_element_type=F32)
                held_now.append((v, q, g, s, d.astype(BF).astype(F32)))
            ready = []
            for v, q, g, s, d in held_now:
                e = jnp.exp(s - jnp.max(s, axis=0, keepdims=True))
                w = e * (1.0 / jnp.sum(e, axis=0, keepdims=True))
                ds = w * (d - jnp.sum(d * w, axis=0, keepdims=True)) * scale
                ready.append((v, q, g, w.astype(BF), ds.astype(BF)))
            for u, (v, q, g, w, ds) in zip(us, ready):
                o = lax.dot_general(w, v, FIRST, preferred_element_type=F32)
                o = jnp.concatenate([o[:GROUP, :HEAD], o[GROUP:, HEAD:]], axis=1).astype(BF)
                dk = jnp.dot(ds, q, preferred_element_type=F32).astype(BF)
                dv = jnp.dot(w, g, preferred_element_type=F32).astype(BF)
                for h, a in enumerate(key_rows(u)):
                    dkv[0, a, :] = dk[h * per_group : (h + 1) * per_group]
                    dkv[1, a, :] = dv[h * per_group : (h + 1) * per_group]
                end = pl.ds(pl.multiple_of(u * GROUP + GROUP - ROWS, ROWS), ROWS)
                os[p, end, :] = jnp.where(last_row, o[GROUP - ROWS :], os[p, end, :])
                os[p, pl.ds(pl.multiple_of((u + 1) * GROUP, GROUP), GROUP), :] = o
            return 0
        lax.fori_loop(0, groups // TOGETHER, several, 0)

    def att_copies(p):
        return [
            pltpu.make_async_remote_copy(
                src_ref=os.at[p, pl.ds(pl.multiple_of(peer * own_rows, own_rows), own_rows), :],
                dst_ref=att_hbm.at[:, head_cols(nbr, p)],
                send_sem=att_send.at[p, k], recv_sem=att_recv.at[p, k],
                device_id=(dp, peer), device_id_type=MESH,
            )
            for k, peer in enumerate(nbr_peers)
        ]

    def att_local(p):
        return pltpu.make_async_copy(
            os.at[p, own_at, :], att_hbm.at[:, head_cols(nbr, p)], att_own.at[p]
        )

    def weight_grads(p):
        for t in range(2):
            got = jnp.dot(enc_t[...], dkv[t], preferred_element_type=F32)
            dw[p, :, :, t * PAIR : (t + 1) * PAIR] = got.reshape(n_dp, width // n_dp, PAIR)

    block = width // n_dp
    total = 2 * PAIR
    cut = part_a.shape[-1]
    mine = [(me // (1 << b)) % 2 for b in range(bits)]

    def partner(b):
        return me + (1 - 2 * mine[b]) * (1 << b)

    pieces = (
        (tuple(range(bits)), slice(0, cut), part_a, send_a, land_a, ra_send, ra_recv),
        (tuple(range(1, bits)) + (0,), slice(cut, total), part_b, send_b, land_b, rb_send, rb_recv),
    )

    def count_at(k):
        return 1 << (bits - 1 - k)

    def offset_at(k):
        return sum(count_at(j) for j in range(k))

    def current(piece, p, k, a, bit):
        order, cols, part = piece[0], piece[1], piece[2]
        if k == 0:
            d = bit * (1 << order[0])
            for m in range(bits - 1):
                d = d + ((a >> m) & 1) * (1 << order[1 + m])
            return dw[p, d, :, cols]
        return part[p, offset_at(k - 1) + a * 2 + bit]

    def sum_copy(piece, p, k):
        _, _, _, send, land, ssem, rsem = piece
        at = pl.ds(offset_at(k), count_at(k))
        return pltpu.make_async_remote_copy(
            src_ref=send.at[p, at], dst_ref=land.at[p, at],
            send_sem=ssem.at[p, k], recv_sem=rsem.at[p, k],
            device_id=(partner(piece[0][k]), nbr), device_id_type=MESH,
        )

    def sum_send(p, k):
        for piece in pieces:
            bit = mine[piece[0][k]]
            for a in range(count_at(k)):
                piece[3][p, offset_at(k) + a] = current(piece, p, k, a, 1 - bit).astype(BF)
            sum_copy(piece, p, k).start()

    def sum_take(p, k):
        for piece in pieces:
            order, cols, part, _, land, _, _ = piece
            bit = mine[order[k]]
            sum_copy(piece, p, k).wait_recv()
            for a in range(count_at(k)):
                got = current(piece, p, k, a, bit) + land[p, offset_at(k) + a].astype(F32)
                if k < bits - 1:
                    part[p, offset_at(k) + a] = got
                else:
                    lo, hi = cols.start, cols.stop
                    for t, out in enumerate((gk_ref, gv_ref)):
                        a0, a1 = max(lo, t * PAIR), min(hi, (t + 1) * PAIR)
                        if a0 < a1:
                            base = p * PAIR - t * PAIR
                            out[:, base + a0 : base + a1] = got[:, a0 - lo : a1 - lo]

    def sum_step(p, k):
        sum_take(p, k)
        if k + 1 < bits:
            sum_send(p, k + 1)

    for p in range(pairs):
        for c in qg_copies(p):
            c.wait_recv()
        for c in qg_local(p):
            c.wait()
        project(p)
        attend(p)
        start(att_copies(p))
        att_local(p).start()
        weight_grads(p)
        sum_send(p, 0)
        for k in range(bits):
            if p - 1 - k >= 0:
                sum_step(p - 1 - k, k)
    for late in range(bits):
        for k in range(late, bits):
            sum_step(pairs - 1 - k + late, k)

    for p in range(pairs):
        for c in att_copies(p):
            c.wait_recv()
            c.wait_send()
        att_local(p).wait()
        for c in qg_copies(p):
            c.wait_send()
        for piece in pieces:
            for k in range(bits):
                sum_copy(piece, p, k).wait_send()
    for h in range(halves):
        for c in a2a_copies(h) + spread(h) + [forward(h)]:
            c.wait_send()


QG_FIRST = 2
TILE_GROUPS = 4
TOGETHER = 3


def fused(queries, cotangent, pool, enc_gain, enc_weight, k_weight, v_weight, owner, slot):
    n_dp, n_nbr = lax.axis_size("dp"), lax.axis_size("nbr")
    held, tokens, width = pool.shape
    own_rows, model = queries.shape
    groups = owner.shape[0] // n_dp
    halves = tokens // ROWS
    pairs = k_weight.shape[1] // PAIR
    bits = n_dp.bit_length() - 1
    block = width // n_dp
    keys = groups * n_nbr * tokens
    steps = (1 << bits) - 1
    cut = 3 * HEAD
    rest = 2 * PAIR - cut
    code = (owner * held + slot).reshape(-1)
    anywhere = pl.BlockSpec(memory_space=pl.ANY)
    vmem = pl.BlockSpec(memory_space=pltpu.VMEM)
    dma = pltpu.SemaphoreType.DMA
    out = pl.pallas_call(
        fused_body,
        in_specs=[pl.BlockSpec(memory_space=pltpu.SMEM), vmem] + [anywhere] * 6,
        out_specs=[anywhere, vmem, vmem],
        out_shape=[
            jax.ShapeDtypeStruct(queries.shape, BF),
            jax.ShapeDtypeStruct((block, k_weight.shape[1]), F32),
            jax.ShapeDtypeStruct((block, v_weight.shape[1]), F32),
        ],
        scratch_shapes=[
            pltpu.VMEM(pool.shape, BF),
            pltpu.VMEM(enc_weight.shape, BF),
            pltpu.VMEM((2,) + k_weight.shape, BF),
            pltpu.VMEM((halves, held, ROWS, width), BF),
            pltpu.VMEM((halves, n_dp, CAP, ROWS, width), BF),
            [pltpu.VMEM((n_dp * CAP, ROWS, width), BF)] * halves,
            pltpu.VMEM((halves, groups, n_nbr, ROWS, width), BF),
            pltpu.VMEM((width, keys), BF),
            pltpu.VMEM((pairs, (groups + 1) * GROUP, PAIR), BF),
            pltpu.VMEM((pairs, (groups + 1) * GROUP, PAIR), BF),
            pltpu.VMEM((pairs, (groups + 1) * GROUP, PAIR), BF),
            pltpu.VMEM((2, keys, PAIR), BF),
            pltpu.VMEM((2, keys, PAIR), BF),
            pltpu.VMEM((pairs, n_dp, block, 2 * PAIR), F32),
            pltpu.VMEM((pairs, steps, block, cut), F32),
            pltpu.VMEM((pairs, steps, block, cut), BF),
            pltpu.VMEM((pairs, steps, block, cut), BF),
            pltpu.VMEM((pairs, steps, block, rest), F32),
            pltpu.VMEM((pairs, steps, block, rest), BF),
            pltpu.VMEM((pairs, steps, block, rest), BF),
            dma((4,)),
            dma((pairs, 2, 3)), dma((pairs, 2, 3)), dma((pairs, 2)),
            dma((halves, n_dp - 1)), dma((halves, n_dp - 1)),
            dma((halves, 3)), dma((halves, 3)),
            dma((pairs, 3)), dma((pairs, 3)), dma((pairs,)),
            dma((pairs, bits)), dma((pairs, bits)), dma((pairs, bits)), dma((pairs, bits)),
        ],
        compiler_params=pltpu.CompilerParams(
            collective_id=0, has_side_effects=True, vmem_limit_bytes=58 * 2**20
        ),
    )(code, enc_gain.reshape(1, -1), queries, cotangent, pool, enc_weight, k_weight, v_weight)
    return tuple(out)


def per_device(
    queries, cotangent, pool, enc_gain, enc_weight, k_weight, v_weight, nbr_owner, nbr_slot
):
    n_dp, n_nbr = lax.axis_size("dp"), lax.axis_size("nbr")
    _, tokens, width = pool.shape
    groups = nbr_owner.shape[0] // n_dp
    args = (
        queries, cotangent, pool, enc_gain, enc_weight, k_weight, v_weight, nbr_owner, nbr_slot
    )
    fits = (
        n_nbr == 4
        and n_dp & (n_dp - 1) == 0
        and width % (n_dp * ROWS) == 0
        and tokens % ROWS == 0
        and k_weight.shape[1] % PAIR == 0
        and groups % TILE_GROUPS == 0
        and groups % TOGETHER == 0
        and HEAD % (n_nbr * ROWS) == 0
    )
    return fused(*args) if fits else staged(*args)


def solution(mesh):
    return jax.shard_map(
        per_device,
        mesh=mesh,
        in_specs=(
            P(("dp", "nbr"), None),
            P(("dp", "nbr"), None),
            P("dp", "nbr", None),
            P(),
            P(),
            P(None, "nbr"),
            P(None, "nbr"),
            P(),
            P(),
        ),
        out_specs=(P(("dp", "nbr"), None), P("dp", "nbr"), P("dp", "nbr")),
        check_vma=False,
    )
```

```python
import jax
import jax.numpy as jnp
from jax import lax
from jax.experimental import pallas as pl
from jax.experimental.pallas import tpu as pltpu
from jax.sharding import PartitionSpec as P

HEAD = 128
GROUP = 64
CAP = 2
BF = jnp.bfloat16
F32 = jnp.float32


def encode(blocks, gain_vec, weight):
    widened = blocks.astype(F32)
    mean_sq = jnp.mean(widened * widened, axis=-1, keepdims=True)
    normed = (widened * lax.rsqrt(mean_sq + 1e-06) * gain_vec).astype(BF)
    combined = jnp.dot(normed, weight, preferred_element_type=F32)
    return (widened + jax.nn.gelu(combined)).astype(BF)


def pick_rows(chosen, rows, tokens):
    m, n = chosen.shape
    eye = jnp.eye(tokens, dtype=BF)
    full = chosen.astype(BF)[:, None, :, None] * eye[None, :, None, :]
    full = full.reshape(m * tokens, n * tokens)
    return jnp.dot(full, rows, preferred_element_type=F32).astype(BF)


def attention_body(q_ref, g_ref, k_ref, v_ref, o_ref, dk_ref, dv_ref):
    heads = q_ref.shape[1] // HEAD
    parts, _, tokens, _ = k_ref.shape
    keys = parts * tokens
    scale = HEAD ** (-0.5)
    over_last = (((1,), (1,)), ((), ()))
    over_first = (((0,), (0,)), ((), ()))
    for first in range(0, heads, 4):
        held = []
        for h in range(first, min(first + 4, heads)):
            cols = slice(h * HEAD, (h + 1) * HEAD)
            k = k_ref[:, 0, :, cols].reshape(keys, HEAD)
            v = v_ref[:, 0, :, cols].reshape(keys, HEAD)
            s = lax.dot_general(q_ref[:, cols], k, over_last, preferred_element_type=F32)
            dw = lax.dot_general(g_ref[:, cols], v, over_last, preferred_element_type=F32)
            held.append((cols, v, s * scale, dw.astype(BF).astype(F32)))
        ready = []
        for cols, v, s, dw in held:
            e = jnp.exp(s - jnp.max(s, axis=-1, keepdims=True))
            p = e * (1.0 / jnp.sum(e, axis=-1, keepdims=True))
            ds = p * (dw - jnp.sum(dw * p, axis=-1, keepdims=True)) * scale
            ready.append((cols, v, p.astype(BF), ds.astype(BF)))
        for cols, v, w, ds in ready:
            q, g = q_ref[:, cols], g_ref[:, cols]
            o_ref[:, cols] = jnp.dot(w, v, preferred_element_type=F32).astype(BF)
            dk = lax.dot_general(ds, q, over_first, preferred_element_type=F32)
            dv = lax.dot_general(w, g, over_first, preferred_element_type=F32)
            dk_ref[:, 0, :, cols] = dk.astype(BF).reshape(parts, tokens, HEAD)
            dv_ref[:, 0, :, cols] = dv.astype(BF).reshape(parts, tokens, HEAD)


def attention(q, g, k, v):
    length, width = q.shape
    parts, groups, tokens, _ = k.shape
    row = pl.BlockSpec((GROUP, width), lambda c: (c, 0))
    block = pl.BlockSpec((parts, 1, tokens, width), lambda c: (0, c, 0, 0))
    work = 10 * length * parts * tokens * width
    return pl.pallas_call(
        attention_body,
        grid=(groups,),
        in_specs=[row, row, block, block],
        out_specs=[row, block, block],
        out_shape=[
            jax.ShapeDtypeStruct(q.shape, BF),
            jax.ShapeDtypeStruct(k.shape, BF),
            jax.ShapeDtypeStruct(v.shape, BF),
        ],
        compiler_params=pltpu.CompilerParams(vmem_limit_bytes=32 * 2**20),
        cost_estimate=pl.CostEstimate(
            flops=work,
            bytes_accessed=6 * length * width + 8 * k.size,
            transcendentals=length * parts * tokens * width // HEAD,
        ),
    )(q, g, k, v)


def exchange(x, axis, split, join):
    n = lax.axis_size(axis)
    me = lax.axis_index(axis)
    span = x.shape[split] // n
    step = x.shape[join]
    parts = []
    for d in range(n):
        piece = lax.dynamic_slice_in_dim(x, (me ^ d) * span, span, split)
        if d:
            piece = lax.ppermute(piece, axis, [(i, i ^ d) for i in range(n)])
        parts.append(piece)
    shape = list(parts[0].shape)
    shape[join] = n * step
    whole = jnp.zeros(shape, x.dtype)
    for d, piece in enumerate(parts):
        whole = lax.dynamic_update_slice_in_dim(whole, piece, (me ^ d) * step, join)
    return whole


def halving(total, axis, turn):
    n = lax.axis_size(axis)
    me = lax.axis_index(axis)
    count = n.bit_length() - 1
    bits = [(i + turn) % count for i in range(count)]
    rows, width = total.shape
    current = total.reshape((2,) * count + (rows // n, width))
    left = list(range(count - 1, -1, -1))
    for bit in bits:
        place = left.index(bit)
        left.pop(place)
        mine = (me >> bit) & 1
        away = lax.dynamic_index_in_dim(current, 1 - mine, place, keepdims=False)
        keep = lax.dynamic_index_in_dim(current, mine, place, keepdims=False)
        pairs = [(i, i ^ (1 << bit)) for i in range(n)]
        current = keep + lax.ppermute(away.astype(BF), axis, pairs).astype(F32)
    return current


def staged(
    queries, cotangent, pool, enc_gain, enc_weight, k_weight, v_weight, nbr_owner, nbr_slot
):
    dp_count = lax.axis_size("dp")
    nbr_count = lax.axis_size("nbr")
    me = lax.axis_index("dp")
    held, tokens, enc_width = pool.shape
    per_row = nbr_owner.shape[0] // dp_count

    owners = nbr_owner[:, 0].reshape(dp_count, per_row)
    slots = nbr_slot[:, 0].reshape(dp_count, per_row)
    same = owners[:, :, None] == owners[:, None, :]
    earlier = jnp.tril(jnp.ones((per_row, per_row), jnp.bool_), -1)
    rank = jnp.sum((same & earlier[None]).astype(jnp.int32), axis=-1)

    ranks = jnp.arange(CAP, dtype=jnp.int32)
    blocks = jnp.arange(held, dtype=jnp.int32)
    mine = (owners == me)[:, None, :] & (rank[:, None, :] == ranks[None, :, None])
    send = jnp.any(
        mine[:, :, None, :] & (slots[:, None, None, :] == blocks[None, None, :, None]), axis=-1
    ).reshape(dp_count * CAP, held)
    enc = encode(pool.reshape(held * tokens, enc_width), enc_gain, enc_weight)
    outgoing = pick_rows(send, enc, tokens)
    arrived = lax.all_to_all(outgoing, "dp", split_axis=0, concat_axis=0, tiled=True)

    q_rows = exchange(queries, "nbr", 1, 0)
    arrived, q_rows = lax.optimization_barrier((arrived, q_rows))

    place = lax.dynamic_slice_in_dim(owners * CAP + rank, me, 1, 0)[0]
    take = place[:, None] == jnp.arange(dp_count * CAP, dtype=jnp.int32)[None, :]
    picked = pick_rows(take, arrived, tokens)
    flat_enc = lax.all_gather(picked, "nbr", axis=0, tiled=True)

    g_rows = exchange(cotangent, "nbr", 1, 0)
    seq_len, width = q_rows.shape
    lead = GROUP - 1
    blank = jnp.zeros((lead, width), BF)
    q_rows = jnp.concatenate([q_rows[lead:], blank], axis=0)
    g_rows = jnp.concatenate([g_rows[lead:], blank], axis=0)

    shape4 = (nbr_count, per_row, tokens, width)
    keys = jnp.dot(flat_enc, k_weight, preferred_element_type=F32).astype(BF)
    values = jnp.dot(flat_enc, v_weight, preferred_element_type=F32).astype(BF)
    out, dk, dv = attention(q_rows, g_rows, keys.reshape(shape4), values.reshape(shape4))

    over_first = (((0,), (0,)), ((), ()))

    def weight_grad(grads):
        return lax.dot_general(
            flat_enc, grads.reshape(-1, width), over_first, preferred_element_type=F32
        )

    grad_v = halving(weight_grad(dv), "dp", 0)
    product_k = weight_grad(dk)
    cut = width // HEAD * 3 // 8 * HEAD
    grad_k = jnp.concatenate(
        [halving(product_k[:, :cut], "dp", 0), halving(product_k[:, cut:], "dp", 1)], axis=1
    )
    out = jnp.concatenate([blank, out[: seq_len - lead]], axis=0)
    merged = exchange(out, "nbr", 0, 1)
    return (merged, grad_k, grad_v)


MESH = pl.DeviceIdType.MESH
ROWS = 16
PAIR = 2 * HEAD
LAST = (((1,), (1,)), ((), ()))
FIRST = (((0,), (0,)), ((), ()))


def gelu(x):
    return jax.nn.gelu(x)


def fused_body(
    code_ref, gain_ref, q_hbm, g_hbm, pool_hbm, encw_hbm, wk_hbm, wv_hbm,
    att_hbm, gk_ref, gv_ref,
    pool_v, encw_v, w_v, local, outbox, inboxes, enc, enc_t, qs, gs, os,
    kv, dkv, dw, part_a, send_a, land_a, part_b, send_b, land_b,
    load_sem, qg_send, qg_recv, qg_own, a2a_send, a2a_recv, gat_send, gat_recv,
    att_send, att_recv, att_own, ra_send, ra_recv, rb_send, rb_recv,
):
    n_dp, n_nbr = lax.axis_size("dp"), lax.axis_size("nbr")
    dp, nbr = lax.axis_index("dp"), lax.axis_index("nbr")
    halves, held, _, width = local.shape
    groups = enc.shape[1]
    pairs, _, _ = qs.shape
    own_rows = q_hbm.shape[0]
    keys = groups * n_nbr * ROWS
    per_group = n_nbr * ROWS
    bits = n_dp.bit_length() - 1

    chip, core = nbr // 2, nbr % 2
    mate = chip * 2 + (1 - core)
    across = ((chip + 1) * 2) % n_nbr + core
    diagonal = ((chip + 1) * 2) % n_nbr + (1 - core)
    nbr_peers = (across, diagonal, mate)
    dp_peers = [(dp + k) % n_dp for k in range(1, n_dp)]

    loads = [
        pltpu.make_async_copy(pool_hbm, pool_v, load_sem.at[0]),
        pltpu.make_async_copy(encw_hbm, encw_v, load_sem.at[1]),
        pltpu.make_async_copy(wk_hbm, w_v.at[0], load_sem.at[2]),
        pltpu.make_async_copy(wv_hbm, w_v.at[1], load_sem.at[3]),
    ]
    loads[0].start()
    loads[1].start()

    barrier = pltpu.get_barrier_semaphore()
    for peer in nbr_peers:
        pl.semaphore_signal(barrier, inc=1, device_id=(dp, peer), device_id_type=MESH)
    for peer in dp_peers:
        pl.semaphore_signal(barrier, inc=1, device_id=(peer, nbr), device_id_type=MESH)
    pl.semaphore_wait(barrier, len(nbr_peers) + len(dp_peers))

    own_at = pl.ds(pl.multiple_of(nbr * own_rows, own_rows), own_rows)

    def head_cols(peer, p):
        return pl.ds(pl.multiple_of((peer * pairs + p) * PAIR, PAIR), PAIR)

    def qg_copies(p):
        made = []
        for t, (src, dst) in enumerate(((q_hbm, qs), (g_hbm, gs))):
            for k, peer in enumerate(nbr_peers):
                made.append(
                    pltpu.make_async_remote_copy(
                        src_ref=src.at[:, head_cols(peer, p)],
                        dst_ref=dst.at[p, own_at, :],
                        send_sem=qg_send.at[p, t, k],
                        recv_sem=qg_recv.at[p, t, k],
                        device_id=(dp, peer),
                        device_id_type=MESH,
                    )
                )
        return made

    def qg_local(p):
        return [
            pltpu.make_async_copy(
                src.at[:, head_cols(nbr, p)], dst.at[p, own_at, :], qg_own.at[p, t]
            )
            for t, (src, dst) in enumerate(((q_hbm, qs), (g_hbm, gs)))
        ]

    def start(copies):
        for c in copies:
            c.start()

    for p in range(QG_FIRST):
        start(qg_copies(p))
    loads[2].start()
    loads[3].start()
    for p in range(pairs):
        start(qg_local(p))

    me = dp

    def chosen_for(s):
        count = jnp.int32(0)
        picks = [jnp.int32(0)] * CAP
        for u in range(groups):
            code = code_ref[s * groups + u]
            hit = code // held == me
            for r in range(CAP):
                picks[r] = jnp.where(hit & (count == r), code % held, picks[r])
            count = count + jnp.where(hit, 1, 0)
        return picks

    chosen = [chosen_for(s) for s in range(n_dp)]
    owners = [code_ref[me * groups + u] // held for u in range(groups)]
    places = []
    for u in range(groups):
        rank = jnp.int32(0)
        for w in range(u):
            rank = rank + jnp.where(owners[w] == owners[u], 1, 0)
        places.append(owners[u] * CAP + rank)

    def a2a_copies(h):
        return [
            pltpu.make_async_remote_copy(
                src_ref=outbox.at[h, peer],
                dst_ref=inboxes[h].at[pl.ds(pl.multiple_of(me * CAP, CAP), CAP)],
                send_sem=a2a_send.at[h, k],
                recv_sem=a2a_recv.at[h, k],
                device_id=(peer, nbr),
                device_id_type=MESH,
            )
            for k, peer in enumerate(dp_peers)
        ]

    loads[0].wait()
    loads[1].wait()
    for h in range(halves):
        x = pool_v[:, h * ROWS : (h + 1) * ROWS, :].reshape(held * ROWS, width).astype(F32)
        mean_sq = jnp.mean(x * x, axis=-1, keepdims=True)
        normed = (x * lax.rsqrt(mean_sq + 1e-06) * gain_ref[...].reshape(1, width)).astype(BF)
        combined = jnp.dot(normed, encw_v[...], preferred_element_type=F32)
        local[h] = (x + gelu(combined)).astype(BF).reshape(held, ROWS, width)
        for s in range(n_dp):
            for r in range(CAP):
                outbox[h, s, r] = local[h, chosen[s][r]]
        start(a2a_copies(h))
        for r in range(CAP):
            inboxes[h][me * CAP + r] = outbox[h, me, r]

    tail = jnp.zeros((GROUP, PAIR), BF)
    for p in range(pairs):
        qs[p, groups * GROUP : (groups + 1) * GROUP, :] = tail
        gs[p, groups * GROUP : (groups + 1) * GROUP, :] = tail
        os[p, 0:GROUP, :] = tail

    def spread(h):
        part = enc.at[h, :, nbr]
        return [
            pltpu.make_async_remote_copy(
                src_ref=part, dst_ref=part,
                send_sem=gat_send.at[h, k], recv_sem=gat_recv.at[h, k],
                device_id=(dp, peer), device_id_type=MESH,
            )
            for k, peer in enumerate((across, mate))
        ]

    def forward(h):
        part = enc.at[h, :, across]
        return pltpu.make_async_remote_copy(
            src_ref=part, dst_ref=part,
            send_sem=gat_send.at[h, 2], recv_sem=gat_recv.at[h, 2],
            device_id=(dp, mate), device_id_type=MESH,
        )

    def transpose(h):
        step = HEAD // per_group
        for u in range(0, groups, step):
            at = h * groups * per_group + u * per_group
            block = enc[h, u : u + step].reshape(HEAD, width)
            enc_t[:, at : at + HEAD] = block.T

    for h in range(halves):
        for c in a2a_copies(h):
            c.wait_recv()
        for u in range(groups):
            enc[h, u, nbr] = inboxes[h][places[u]]
        start(spread(h))
    for h in range(halves):
        spread(h)[0].wait_recv()
        forward(h).start()
        spread(h)[1].wait_recv()
        forward(h).wait_recv()
        transpose(h)
    for p in range(QG_FIRST, pairs):
        start(qg_copies(p))
    loads[2].wait()
    loads[3].wait()

    def project(p):
        cols = slice(p * PAIR, (p + 1) * PAIR)
        for h in range(halves):
            def tile(i, _):
                u = i * TILE_GROUPS
                rows = TILE_GROUPS * per_group
                e = enc[h, pl.ds(u, TILE_GROUPS)].reshape(rows, width)
                at = pl.ds(pl.multiple_of(h * groups * per_group + u * per_group, rows), rows)
                for t in range(2):
                    kv[t, at, :] = jnp.dot(
                        e, w_v[t, :, cols], preferred_element_type=F32
                    ).astype(BF)
                return 0
            lax.fori_loop(0, groups // TILE_GROUPS, tile, 0)

    scale = HEAD ** (-0.5)
    last_row = lax.broadcasted_iota(jnp.int32, (ROWS, PAIR), 0) == ROWS - 1
    blank = jnp.zeros((GROUP, HEAD), BF)

    def rows_of(ref, p, u):
        here = ref[p, pl.ds(pl.multiple_of(u * GROUP + GROUP - ROWS, ROWS), ROWS), :]
        after = ref[p, pl.ds(pl.multiple_of((u + 1) * GROUP, GROUP), GROUP), :]
        end = jnp.where(last_row, here, after[GROUP - ROWS :])
        got = jnp.concatenate([after[: GROUP - ROWS], end], axis=0)
        return jnp.concatenate(
            [
                jnp.concatenate([got[:, :HEAD], blank], axis=1),
                jnp.concatenate([blank, got[:, HEAD:]], axis=1),
            ],
            axis=0,
        )

    def key_rows(u):
        return [
            pl.ds(pl.multiple_of(h * groups * per_group + u * per_group, per_group), per_group)
            for h in range(halves)
        ]

    def attend(p):
        def several(i, _):
            us = [i * TOGETHER + j for j in range(TOGETHER)]
            held_now = []
            for u in us:
                at = key_rows(u)
                k = jnp.concatenate([kv[0, a, :] for a in at], axis=0)
                v = jnp.concatenate([kv[1, a, :] for a in at], axis=0)
                q, g = rows_of(qs, p, u), rows_of(gs, p, u)
                s = lax.dot_general(k, q, LAST, preferred_element_type=F32) * scale
                d = lax.dot_general(v, g, LAST, preferred_element_type=F32)
                held_now.append((v, q, g, s, d.astype(BF).astype(F32)))
            ready = []
            for v, q, g, s, d in held_now:
                e = jnp.exp(s - jnp.max(s, axis=0, keepdims=True))
                w = e * (1.0 / jnp.sum(e, axis=0, keepdims=True))
                ds = w * (d - jnp.sum(d * w, axis=0, keepdims=True)) * scale
                ready.append((v, q, g, w.astype(BF), ds.astype(BF)))
            for u, (v, q, g, w, ds) in zip(us, ready):
                o = lax.dot_general(w, v, FIRST, preferred_element_type=F32)
                o = jnp.concatenate([o[:GROUP, :HEAD], o[GROUP:, HEAD:]], axis=1).astype(BF)
                dk = jnp.dot(ds, q, preferred_element_type=F32).astype(BF)
                dv = jnp.dot(w, g, preferred_element_type=F32).astype(BF)
                for h, a in enumerate(key_rows(u)):
                    dkv[0, a, :] = dk[h * per_group : (h + 1) * per_group]
                    dkv[1, a, :] = dv[h * per_group : (h + 1) * per_group]
                end = pl.ds(pl.multiple_of(u * GROUP + GROUP - ROWS, ROWS), ROWS)
                os[p, end, :] = jnp.where(last_row, o[GROUP - ROWS :], os[p, end, :])
                os[p, pl.ds(pl.multiple_of((u + 1) * GROUP, GROUP), GROUP), :] = o
            return 0
        lax.fori_loop(0, groups // TOGETHER, several, 0)

    def att_copies(p):
        return [
            pltpu.make_async_remote_copy(
                src_ref=os.at[p, pl.ds(pl.multiple_of(peer * own_rows, own_rows), own_rows), :],
                dst_ref=att_hbm.at[:, head_cols(nbr, p)],
                send_sem=att_send.at[p, k], recv_sem=att_recv.at[p, k],
                device_id=(dp, peer), device_id_type=MESH,
            )
            for k, peer in enumerate(nbr_peers)
        ]

    def att_local(p):
        return pltpu.make_async_copy(
            os.at[p, own_at, :], att_hbm.at[:, head_cols(nbr, p)], att_own.at[p]
        )

    def weight_grads(p):
        for t in range(2):
            got = jnp.dot(enc_t[...], dkv[t], preferred_element_type=F32)
            dw[p, :, :, t * PAIR : (t + 1) * PAIR] = got.reshape(n_dp, width // n_dp, PAIR)

    block = width // n_dp
    total = 2 * PAIR
    cut = part_a.shape[-1]
    mine = [(me // (1 << b)) % 2 for b in range(bits)]

    def partner(b):
        return me + (1 - 2 * mine[b]) * (1 << b)

    pieces = (
        (tuple(range(bits)), slice(0, cut), part_a, send_a, land_a, ra_send, ra_recv),
        (tuple(range(1, bits)) + (0,), slice(cut, total), part_b, send_b, land_b, rb_send, rb_recv),
    )

    def count_at(k):
        return 1 << (bits - 1 - k)

    def offset_at(k):
        return sum(count_at(j) for j in range(k))

    def current(piece, p, k, a, bit):
        order, cols, part = piece[0], piece[1], piece[2]
        if k == 0:
            d = bit * (1 << order[0])
            for m in range(bits - 1):
                d = d + ((a >> m) & 1) * (1 << order[1 + m])
            return dw[p, d, :, cols]
        return part[p, offset_at(k - 1) + a * 2 + bit]

    def sum_copy(piece, p, k):
        _, _, _, send, land, ssem, rsem = piece
        at = pl.ds(offset_at(k), count_at(k))
        return pltpu.make_async_remote_copy(
            src_ref=send.at[p, at], dst_ref=land.at[p, at],
            send_sem=ssem.at[p, k], recv_sem=rsem.at[p, k],
            device_id=(partner(piece[0][k]), nbr), device_id_type=MESH,
        )

    def sum_send(p, k):
        for piece in pieces:
            bit = mine[piece[0][k]]
            for a in range(count_at(k)):
                piece[3][p, offset_at(k) + a] = current(piece, p, k, a, 1 - bit).astype(BF)
            sum_copy(piece, p, k).start()

    def sum_take(p, k):
        for piece in pieces:
            order, cols, part, _, land, _, _ = piece
            bit = mine[order[k]]
            sum_copy(piece, p, k).wait_recv()
            for a in range(count_at(k)):
                got = current(piece, p, k, a, bit) + land[p, offset_at(k) + a].astype(F32)
                if k < bits - 1:
                    part[p, offset_at(k) + a] = got
                else:
                    lo, hi = cols.start, cols.stop
                    for t, out in enumerate((gk_ref, gv_ref)):
                        a0, a1 = max(lo, t * PAIR), min(hi, (t + 1) * PAIR)
                        if a0 < a1:
                            base = p * PAIR - t * PAIR
                            out[:, base + a0 : base + a1] = got[:, a0 - lo : a1 - lo]

    def sum_step(p, k):
        sum_take(p, k)
        if k + 1 < bits:
            sum_send(p, k + 1)

    for p in range(pairs):
        for c in qg_copies(p):
            c.wait_recv()
        for c in qg_local(p):
            c.wait()
        project(p)
        attend(p)
        start(att_copies(p))
        att_local(p).start()
        weight_grads(p)
        sum_send(p, 0)
        for k in range(bits):
            if p - 1 - k >= 0:
                sum_step(p - 1 - k, k)
    for late in range(bits):
        for k in range(late, bits):
            sum_step(pairs - 1 - k + late, k)

    for p in range(pairs):
        for c in att_copies(p):
            c.wait_recv()
            c.wait_send()
        att_local(p).wait()
        for c in qg_copies(p):
            c.wait_send()
        for piece in pieces:
            for k in range(bits):
                sum_copy(piece, p, k).wait_send()
    for h in range(halves):
        for c in a2a_copies(h) + spread(h) + [forward(h)]:
            c.wait_send()


QG_FIRST = 1
TILE_GROUPS = 4
TOGETHER = 3


def fused(queries, cotangent, pool, enc_gain, enc_weight, k_weight, v_weight, owner, slot):
    n_dp, n_nbr = lax.axis_size("dp"), lax.axis_size("nbr")
    held, tokens, width = pool.shape
    own_rows, model = queries.shape
    groups = owner.shape[0] // n_dp
    halves = tokens // ROWS
    pairs = k_weight.shape[1] // PAIR
    bits = n_dp.bit_length() - 1
    block = width // n_dp
    keys = groups * n_nbr * tokens
    steps = (1 << bits) - 1
    cut = 3 * HEAD
    rest = 2 * PAIR - cut
    code = (owner * held + slot).reshape(-1)
    anywhere = pl.BlockSpec(memory_space=pl.ANY)
    vmem = pl.BlockSpec(memory_space=pltpu.VMEM)
    dma = pltpu.SemaphoreType.DMA
    out = pl.pallas_call(
        fused_body,
        in_specs=[pl.BlockSpec(memory_space=pltpu.SMEM), vmem] + [anywhere] * 6,
        out_specs=[anywhere, vmem, vmem],
        out_shape=[
            jax.ShapeDtypeStruct(queries.shape, BF),
            jax.ShapeDtypeStruct((block, k_weight.shape[1]), F32),
            jax.ShapeDtypeStruct((block, v_weight.shape[1]), F32),
        ],
        scratch_shapes=[
            pltpu.VMEM(pool.shape, BF),
            pltpu.VMEM(enc_weight.shape, BF),
            pltpu.VMEM((2,) + k_weight.shape, BF),
            pltpu.VMEM((halves, held, ROWS, width), BF),
            pltpu.VMEM((halves, n_dp, CAP, ROWS, width), BF),
            [pltpu.VMEM((n_dp * CAP, ROWS, width), BF)] * halves,
            pltpu.VMEM((halves, groups, n_nbr, ROWS, width), BF),
            pltpu.VMEM((width, keys), BF),
            pltpu.VMEM((pairs, (groups + 1) * GROUP, PAIR), BF),
            pltpu.VMEM((pairs, (groups + 1) * GROUP, PAIR), BF),
            pltpu.VMEM((pairs, (groups + 1) * GROUP, PAIR), BF),
            pltpu.VMEM((2, keys, PAIR), BF),
            pltpu.VMEM((2, keys, PAIR), BF),
            pltpu.VMEM((pairs, n_dp, block, 2 * PAIR), F32),
            pltpu.VMEM((pairs, steps, block, cut), F32),
            pltpu.VMEM((pairs, steps, block, cut), BF),
            pltpu.VMEM((pairs, steps, block, cut), BF),
            pltpu.VMEM((pairs, steps, block, rest), F32),
            pltpu.VMEM((pairs, steps, block, rest), BF),
            pltpu.VMEM((pairs, steps, block, rest), BF),
            dma((4,)),
            dma((pairs, 2, 3)), dma((pairs, 2, 3)), dma((pairs, 2)),
            dma((halves, n_dp - 1)), dma((halves, n_dp - 1)),
            dma((halves, 3)), dma((halves, 3)),
            dma((pairs, 3)), dma((pairs, 3)), dma((pairs,)),
            dma((pairs, bits)), dma((pairs, bits)), dma((pairs, bits)), dma((pairs, bits)),
        ],
        compiler_params=pltpu.CompilerParams(
            collective_id=0, has_side_effects=True, vmem_limit_bytes=58 * 2**20
        ),
    )(code, enc_gain, queries, cotangent, pool, enc_weight, k_weight, v_weight)
    return tuple(out)


def per_device(
    queries, cotangent, pool, enc_gain, enc_weight, k_weight, v_weight, nbr_owner, nbr_slot
):
    n_dp, n_nbr = lax.axis_size("dp"), lax.axis_size("nbr")
    _, tokens, width = pool.shape
    groups = nbr_owner.shape[0] // n_dp
    args = (
        queries, cotangent, pool, enc_gain, enc_weight, k_weight, v_weight, nbr_owner, nbr_slot
    )
    fits = (
        n_nbr == 4
        and n_dp & (n_dp - 1) == 0
        and width % (n_dp * ROWS) == 0
        and tokens % ROWS == 0
        and k_weight.shape[1] % PAIR == 0
        and groups % TILE_GROUPS == 0
        and groups % TOGETHER == 0
        and HEAD % (n_nbr * ROWS) == 0
    )
    return fused(*args) if fits else staged(*args)


def solution(mesh):
    return jax.shard_map(
        per_device,
        mesh=mesh,
        in_specs=(
            P(("dp", "nbr"), None),
            P(("dp", "nbr"), None),
            P("dp", "nbr", None),
            P(),
            P(),
            P(None, "nbr"),
            P(None, "nbr"),
            P(),
            P(),
        ),
        out_specs=(P(("dp", "nbr"), None), P("dp", "nbr"), P("dp", "nbr")),
        check_vma=False,
    )
```

```python
import jax
import jax.numpy as jnp
from jax import lax
from jax.experimental import pallas as pl
from jax.experimental.pallas import tpu as pltpu
from jax.sharding import PartitionSpec as P

HEAD = 128
GROUP = 64
CAP = 2
BF = jnp.bfloat16
F32 = jnp.float32


def encode(blocks, gain_vec, weight):
    widened = blocks.astype(F32)
    mean_sq = jnp.mean(widened * widened, axis=-1, keepdims=True)
    normed = (widened * lax.rsqrt(mean_sq + 1e-06) * gain_vec).astype(BF)
    combined = jnp.dot(normed, weight, preferred_element_type=F32)
    return (widened + jax.nn.gelu(combined)).astype(BF)


def pick_rows(chosen, rows, tokens):
    m, n = chosen.shape
    eye = jnp.eye(tokens, dtype=BF)
    full = chosen.astype(BF)[:, None, :, None] * eye[None, :, None, :]
    full = full.reshape(m * tokens, n * tokens)
    return jnp.dot(full, rows, preferred_element_type=F32).astype(BF)


def attention_body(q_ref, g_ref, k_ref, v_ref, o_ref, dk_ref, dv_ref):
    heads = q_ref.shape[1] // HEAD
    parts, _, tokens, _ = k_ref.shape
    keys = parts * tokens
    scale = HEAD ** (-0.5)
    over_last = (((1,), (1,)), ((), ()))
    over_first = (((0,), (0,)), ((), ()))
    for first in range(0, heads, 4):
        held = []
        for h in range(first, min(first + 4, heads)):
            cols = slice(h * HEAD, (h + 1) * HEAD)
            k = k_ref[:, 0, :, cols].reshape(keys, HEAD)
            v = v_ref[:, 0, :, cols].reshape(keys, HEAD)
            s = lax.dot_general(q_ref[:, cols], k, over_last, preferred_element_type=F32)
            dw = lax.dot_general(g_ref[:, cols], v, over_last, preferred_element_type=F32)
            held.append((cols, v, s * scale, dw.astype(BF).astype(F32)))
        ready = []
        for cols, v, s, dw in held:
            e = jnp.exp(s - jnp.max(s, axis=-1, keepdims=True))
            p = e * (1.0 / jnp.sum(e, axis=-1, keepdims=True))
            ds = p * (dw - jnp.sum(dw * p, axis=-1, keepdims=True)) * scale
            ready.append((cols, v, p.astype(BF), ds.astype(BF)))
        for cols, v, w, ds in ready:
            q, g = q_ref[:, cols], g_ref[:, cols]
            o_ref[:, cols] = jnp.dot(w, v, preferred_element_type=F32).astype(BF)
            dk = lax.dot_general(ds, q, over_first, preferred_element_type=F32)
            dv = lax.dot_general(w, g, over_first, preferred_element_type=F32)
            dk_ref[:, 0, :, cols] = dk.astype(BF).reshape(parts, tokens, HEAD)
            dv_ref[:, 0, :, cols] = dv.astype(BF).reshape(parts, tokens, HEAD)


def attention(q, g, k, v):
    length, width = q.shape
    parts, groups, tokens, _ = k.shape
    row = pl.BlockSpec((GROUP, width), lambda c: (c, 0))
    block = pl.BlockSpec((parts, 1, tokens, width), lambda c: (0, c, 0, 0))
    work = 10 * length * parts * tokens * width
    return pl.pallas_call(
        attention_body,
        grid=(groups,),
        in_specs=[row, row, block, block],
        out_specs=[row, block, block],
        out_shape=[
            jax.ShapeDtypeStruct(q.shape, BF),
            jax.ShapeDtypeStruct(k.shape, BF),
            jax.ShapeDtypeStruct(v.shape, BF),
        ],
        compiler_params=pltpu.CompilerParams(vmem_limit_bytes=32 * 2**20),
        cost_estimate=pl.CostEstimate(
            flops=work,
            bytes_accessed=6 * length * width + 8 * k.size,
            transcendentals=length * parts * tokens * width // HEAD,
        ),
    )(q, g, k, v)


def exchange(x, axis, split, join):
    n = lax.axis_size(axis)
    me = lax.axis_index(axis)
    span = x.shape[split] // n
    step = x.shape[join]
    parts = []
    for d in range(n):
        piece = lax.dynamic_slice_in_dim(x, (me ^ d) * span, span, split)
        if d:
            piece = lax.ppermute(piece, axis, [(i, i ^ d) for i in range(n)])
        parts.append(piece)
    shape = list(parts[0].shape)
    shape[join] = n * step
    whole = jnp.zeros(shape, x.dtype)
    for d, piece in enumerate(parts):
        whole = lax.dynamic_update_slice_in_dim(whole, piece, (me ^ d) * step, join)
    return whole


def halving(total, axis, turn):
    n = lax.axis_size(axis)
    me = lax.axis_index(axis)
    count = n.bit_length() - 1
    bits = [(i + turn) % count for i in range(count)]
    rows, width = total.shape
    current = total.reshape((2,) * count + (rows // n, width))
    left = list(range(count - 1, -1, -1))
    for bit in bits:
        place = left.index(bit)
        left.pop(place)
        mine = (me >> bit) & 1
        away = lax.dynamic_index_in_dim(current, 1 - mine, place, keepdims=False)
        keep = lax.dynamic_index_in_dim(current, mine, place, keepdims=False)
        pairs = [(i, i ^ (1 << bit)) for i in range(n)]
        current = keep + lax.ppermute(away.astype(BF), axis, pairs).astype(F32)
    return current


def staged(
    queries, cotangent, pool, enc_gain, enc_weight, k_weight, v_weight, nbr_owner, nbr_slot
):
    dp_count = lax.axis_size("dp")
    nbr_count = lax.axis_size("nbr")
    me = lax.axis_index("dp")
    held, tokens, enc_width = pool.shape
    per_row = nbr_owner.shape[0] // dp_count

    owners = nbr_owner[:, 0].reshape(dp_count, per_row)
    slots = nbr_slot[:, 0].reshape(dp_count, per_row)
    same = owners[:, :, None] == owners[:, None, :]
    earlier = jnp.tril(jnp.ones((per_row, per_row), jnp.bool_), -1)
    rank = jnp.sum((same & earlier[None]).astype(jnp.int32), axis=-1)

    ranks = jnp.arange(CAP, dtype=jnp.int32)
    blocks = jnp.arange(held, dtype=jnp.int32)
    mine = (owners == me)[:, None, :] & (rank[:, None, :] == ranks[None, :, None])
    send = jnp.any(
        mine[:, :, None, :] & (slots[:, None, None, :] == blocks[None, None, :, None]), axis=-1
    ).reshape(dp_count * CAP, held)
    enc = encode(pool.reshape(held * tokens, enc_width), enc_gain, enc_weight)
    outgoing = pick_rows(send, enc, tokens)
    arrived = lax.all_to_all(outgoing, "dp", split_axis=0, concat_axis=0, tiled=True)

    q_rows = exchange(queries, "nbr", 1, 0)
    arrived, q_rows = lax.optimization_barrier((arrived, q_rows))

    place = lax.dynamic_slice_in_dim(owners * CAP + rank, me, 1, 0)[0]
    take = place[:, None] == jnp.arange(dp_count * CAP, dtype=jnp.int32)[None, :]
    picked = pick_rows(take, arrived, tokens)
    flat_enc = lax.all_gather(picked, "nbr", axis=0, tiled=True)

    g_rows = exchange(cotangent, "nbr", 1, 0)
    seq_len, width = q_rows.shape
    lead = GROUP - 1
    blank = jnp.zeros((lead, width), BF)
    q_rows = jnp.concatenate([q_rows[lead:], blank], axis=0)
    g_rows = jnp.concatenate([g_rows[lead:], blank], axis=0)

    shape4 = (nbr_count, per_row, tokens, width)
    keys = jnp.dot(flat_enc, k_weight, preferred_element_type=F32).astype(BF)
    values = jnp.dot(flat_enc, v_weight, preferred_element_type=F32).astype(BF)
    out, dk, dv = attention(q_rows, g_rows, keys.reshape(shape4), values.reshape(shape4))

    over_first = (((0,), (0,)), ((), ()))

    def weight_grad(grads):
        return lax.dot_general(
            flat_enc, grads.reshape(-1, width), over_first, preferred_element_type=F32
        )

    grad_v = halving(weight_grad(dv), "dp", 0)
    product_k = weight_grad(dk)
    cut = width // HEAD * 3 // 8 * HEAD
    grad_k = jnp.concatenate(
        [halving(product_k[:, :cut], "dp", 0), halving(product_k[:, cut:], "dp", 1)], axis=1
    )
    out = jnp.concatenate([blank, out[: seq_len - lead]], axis=0)
    merged = exchange(out, "nbr", 0, 1)
    return (merged, grad_k, grad_v)


MESH = pl.DeviceIdType.MESH
ROWS = 16
PAIR = 2 * HEAD
LAST = (((1,), (1,)), ((), ()))
FIRST = (((0,), (0,)), ((), ()))


def gelu(x):
    return jax.nn.gelu(x)


def fused_body(
    code_ref, gain_ref, q_hbm, g_hbm, pool_hbm, encw_hbm, wk_hbm, wv_hbm,
    att_hbm, gk_ref, gv_ref,
    pool_v, encw_v, w_v, local, outboxes, inboxes, enc, enc_t, qs, gs, os,
    kv, dkv, dw, parts_a, sends_a, lands_a, parts_b, sends_b, lands_b,
    load_sem, qg_send, qg_recv, qg_own, a2a_send, a2a_recv, gat_send, gat_recv,
    att_send, att_recv, att_own, ra_send, ra_recv, rb_send, rb_recv,
):
    n_dp, n_nbr = lax.axis_size("dp"), lax.axis_size("nbr")
    dp, nbr = lax.axis_index("dp"), lax.axis_index("nbr")
    held, tokens, width = pool_v.shape
    halves, groups = enc.shape[:2]
    cuts = column_cuts(halves, width)
    pairs, _, _ = qs.shape
    own_rows = q_hbm.shape[0]
    keys = groups * n_nbr * ROWS
    per_group = n_nbr * ROWS
    bits = n_dp.bit_length() - 1

    chip, core = nbr // 2, nbr % 2
    mate = chip * 2 + (1 - core)
    across = ((chip + 1) * 2) % n_nbr + core
    diagonal = ((chip + 1) * 2) % n_nbr + (1 - core)
    nbr_peers = (across, diagonal, mate)
    dp_peers = [(dp + k) % n_dp for k in range(1, n_dp)]

    loads = [
        pltpu.make_async_copy(pool_hbm, pool_v, load_sem.at[0]),
        pltpu.make_async_copy(encw_hbm, encw_v, load_sem.at[1]),
        pltpu.make_async_copy(wk_hbm, w_v.at[0], load_sem.at[2]),
        pltpu.make_async_copy(wv_hbm, w_v.at[1], load_sem.at[3]),
    ]
    loads[0].start()
    loads[1].start()

    barrier = pltpu.get_barrier_semaphore()
    for peer in nbr_peers:
        pl.semaphore_signal(barrier, inc=1, device_id=(dp, peer), device_id_type=MESH)
    for peer in dp_peers:
        pl.semaphore_signal(barrier, inc=1, device_id=(peer, nbr), device_id_type=MESH)
    own_at = pl.ds(pl.multiple_of(nbr * own_rows, own_rows), own_rows)

    def head_cols(peer, p):
        return pl.ds(pl.multiple_of((peer * pairs + p) * PAIR, PAIR), PAIR)

    def qg_copies(p):
        made = []
        for t, (src, dst) in enumerate(((q_hbm, qs), (g_hbm, gs))):
            for k, peer in enumerate(nbr_peers):
                made.append(
                    pltpu.make_async_remote_copy(
                        src_ref=src.at[:, head_cols(peer, p)],
                        dst_ref=dst.at[p, own_at, :],
                        send_sem=qg_send.at[p, t, k],
                        recv_sem=qg_recv.at[p, t, k],
                        device_id=(dp, peer),
                        device_id_type=MESH,
                    )
                )
        return made

    def qg_local(p):
        return [
            pltpu.make_async_copy(
                src.at[:, head_cols(nbr, p)], dst.at[p, own_at, :], qg_own.at[p, t]
            )
            for t, (src, dst) in enumerate(((q_hbm, qs), (g_hbm, gs)))
        ]

    def start(copies):
        for c in copies:
            c.start()

    me = dp

    def chosen_for(s):
        count = jnp.int32(0)
        picks = [jnp.int32(0)] * CAP
        for u in range(groups):
            code = code_ref[s * groups + u]
            hit = code // held == me
            for r in range(CAP):
                picks[r] = jnp.where(hit & (count == r), code % held, picks[r])
            count = count + jnp.where(hit, 1, 0)
        return picks

    chosen = [chosen_for(s) for s in range(n_dp)]
    owners = [code_ref[me * groups + u] // held for u in range(groups)]
    places = []
    for u in range(groups):
        rank = jnp.int32(0)
        for w in range(u):
            rank = rank + jnp.where(owners[w] == owners[u], 1, 0)
        places.append(owners[u] * CAP + rank)

    def a2a_copies(n):
        return [
            pltpu.make_async_remote_copy(
                src_ref=outboxes[n].at[peer],
                dst_ref=inboxes[n].at[pl.ds(pl.multiple_of(me * CAP, CAP), CAP)],
                send_sem=a2a_send.at[n, k],
                recv_sem=a2a_recv.at[n, k],
                device_id=(peer, nbr),
                device_id_type=MESH,
            )
            for k, peer in enumerate(dp_peers)
        ]

    def encoded(x):
        x = x.astype(F32)
        mean_sq = jnp.mean(x * x, axis=-1, keepdims=True)
        normed = (x * lax.rsqrt(mean_sq + 1e-06) * gain_ref[...].reshape(1, width)).astype(BF)
        combined = jnp.dot(normed, encw_v[...], preferred_element_type=F32)
        return (x + jax.nn.gelu(combined)).astype(BF)

    def fill_outbox(n, block_at):
        for s in range(n_dp):
            for r in range(CAP):
                outboxes[n][s, r] = block_at(chosen[s][r])

    def keep_own(n):
        for r in range(CAP):
            inboxes[n][me * CAP + r] = outboxes[n][me, r]

    loads[0].wait()
    loads[1].wait()
    for h in range(halves):
        x = pool_v[:, h * ROWS : (h + 1) * ROWS, :].reshape(held * ROWS, width)
        local[h] = encoded(x).reshape(held, ROWS, width)
    for n, (h, cols) in enumerate(cuts):
        fill_outbox(n, lambda b: local[h, b, :, cols])
        keep_own(n)
    pl.semaphore_wait(barrier, len(nbr_peers) + len(dp_peers))
    start(a2a_copies(0))
    start(qg_copies(0))
    loads[2].start()
    loads[3].start()
    for p in range(pairs):
        start(qg_local(p))

    tail = jnp.zeros((GROUP, PAIR), BF)
    for p in range(pairs):
        qs[p, groups * GROUP : (groups + 1) * GROUP, :] = tail
        gs[p, groups * GROUP : (groups + 1) * GROUP, :] = tail
        os[p, 0:GROUP, :] = tail

    def spread(n):
        h, cols = cuts[n]
        part = enc.at[h, :, nbr, :, cols]
        return [
            pltpu.make_async_remote_copy(
                src_ref=part, dst_ref=part,
                send_sem=gat_send.at[n, k], recv_sem=gat_recv.at[n, k],
                device_id=(dp, peer), device_id_type=MESH,
            )
            for k, peer in enumerate((across, mate))
        ]

    def forward(n):
        h, cols = cuts[n]
        part = enc.at[h, :, across, :, cols]
        return pltpu.make_async_remote_copy(
            src_ref=part, dst_ref=part,
            send_sem=gat_send.at[n, 2], recv_sem=gat_recv.at[n, 2],
            device_id=(dp, mate), device_id_type=MESH,
        )

    def transpose(h):
        step = HEAD // per_group
        for u in range(0, groups, step):
            at = h * groups * per_group + u * per_group
            block = enc[h, u : u + step].reshape(HEAD, width)
            enc_t[:, at : at + HEAD] = block.T

    if EARLY:
        for c in qg_copies(0):
            c.wait_recv()
        start(qg_copies(1)[:EARLY])
    for n, (h, cols) in enumerate(cuts):
        if n + 1 < len(cuts):
            for c in a2a_copies(n):
                c.wait_send()
            start(a2a_copies(n + 1))
        for c in a2a_copies(n):
            c.wait_recv()
        for u in range(groups):
            enc[h, u, nbr, :, cols] = inboxes[n][places[u]]
        start(spread(n))

    def project(p, hs):
        cols = slice(p * PAIR, (p + 1) * PAIR)
        for h in hs:
            def tile(i, _):
                u = i * TILE_GROUPS
                rows = TILE_GROUPS * per_group
                e = enc[h, pl.ds(u, TILE_GROUPS)].reshape(rows, width)
                at = pl.ds(pl.multiple_of(h * groups * per_group + u * per_group, rows), rows)
                for t in range(2):
                    kv[t, at, :] = jnp.dot(
                        e, w_v[t, :, cols], preferred_element_type=F32
                    ).astype(BF)
                return 0
            lax.fori_loop(0, groups // TILE_GROUPS, tile, 0)

    scale = HEAD ** (-0.5)
    last_row = lax.broadcasted_iota(jnp.int32, (ROWS, PAIR), 0) == ROWS - 1
    blank = jnp.zeros((GROUP, HEAD), BF)

    def rows_of(ref, p, u):
        here = ref[p, pl.ds(pl.multiple_of(u * GROUP + GROUP - ROWS, ROWS), ROWS), :]
        after = ref[p, pl.ds(pl.multiple_of((u + 1) * GROUP, GROUP), GROUP), :]
        end = jnp.where(last_row, here, after[GROUP - ROWS :])
        got = jnp.concatenate([after[: GROUP - ROWS], end], axis=0)
        return jnp.concatenate(
            [
                jnp.concatenate([got[:, :HEAD], blank], axis=1),
                jnp.concatenate([blank, got[:, HEAD:]], axis=1),
            ],
            axis=0,
        )

    def key_rows(u):
        return [
            pl.ds(pl.multiple_of(h * groups * per_group + u * per_group, per_group), per_group)
            for h in range(halves)
        ]

    def attend(p):
        def several(i, _):
            us = [i * TOGETHER + j for j in range(TOGETHER)]
            held_now = []
            for u in us:
                at = key_rows(u)
                k = jnp.concatenate([kv[0, a, :] for a in at], axis=0)
                v = jnp.concatenate([kv[1, a, :] for a in at], axis=0)
                q, g = rows_of(qs, p, u), rows_of(gs, p, u)
                s = lax.dot_general(k, q, LAST, preferred_element_type=F32) * scale
                d = lax.dot_general(v, g, LAST, preferred_element_type=F32)
                held_now.append((v, q, g, s, d.astype(BF).astype(F32)))
            ready = []
            for v, q, g, s, d in held_now:
                e = jnp.exp(s - jnp.max(s, axis=0, keepdims=True))
                w = e * (1.0 / jnp.sum(e, axis=0, keepdims=True))
                ds = w * (d - jnp.sum(d * w, axis=0, keepdims=True)) * scale
                ready.append((v, q, g, w.astype(BF), ds.astype(BF)))
            for u, (v, q, g, w, ds) in zip(us, ready):
                o = lax.dot_general(w, v, FIRST, preferred_element_type=F32)
                o = jnp.concatenate([o[:GROUP, :HEAD], o[GROUP:, HEAD:]], axis=1).astype(BF)
                dk = jnp.dot(ds, q, preferred_element_type=F32).astype(BF)
                dv = jnp.dot(w, g, preferred_element_type=F32).astype(BF)
                for h, a in enumerate(key_rows(u)):
                    dkv[0, a, :] = dk[h * per_group : (h + 1) * per_group]
                    dkv[1, a, :] = dv[h * per_group : (h + 1) * per_group]
                end = pl.ds(pl.multiple_of(u * GROUP + GROUP - ROWS, ROWS), ROWS)
                os[p, end, :] = jnp.where(last_row, o[GROUP - ROWS :], os[p, end, :])
                os[p, pl.ds(pl.multiple_of((u + 1) * GROUP, GROUP), GROUP), :] = o
            return 0
        lax.fori_loop(0, groups // TOGETHER, several, 0)

    def att_copies(p):
        return [
            pltpu.make_async_remote_copy(
                src_ref=os.at[p, pl.ds(pl.multiple_of(peer * own_rows, own_rows), own_rows), :],
                dst_ref=att_hbm.at[:, head_cols(nbr, p)],
                send_sem=att_send.at[p, k], recv_sem=att_recv.at[p, k],
                device_id=(dp, peer), device_id_type=MESH,
            )
            for k, peer in enumerate(nbr_peers)
        ]

    def att_local(p):
        return pltpu.make_async_copy(
            os.at[p, own_at, :], att_hbm.at[:, head_cols(nbr, p)], att_own.at[p]
        )

    def weight_grads(p):
        for t in range(2):
            got = jnp.dot(enc_t[...], dkv[t], preferred_element_type=F32)
            dw[p, :, :, t * PAIR : (t + 1) * PAIR] = got.reshape(n_dp, width // n_dp, PAIR)

    mine = [(me // (1 << b)) % 2 for b in range(bits)]

    def partner(b):
        return me + (1 - 2 * mine[b]) * (1 << b)

    def pieces_of(p):
        made = []
        orders = (tuple(range(bits)), tuple(range(1, bits)) + (0,))
        stacks = ((parts_a, sends_a, lands_a), (parts_b, sends_b, lands_b))
        for n, (lo, hi) in enumerate(((0, CUTS[p]), (CUTS[p], 2 * PAIR))):
            if lo < hi:
                part, send, land = (x[p] for x in stacks[n])
                sems = (ra_send, ra_recv) if n == 0 else (rb_send, rb_recv)
                made.append((orders[n], slice(lo, hi), part, send, land) + sems)
        return made

    def count_at(k):
        return 1 << (bits - 1 - k)

    def offset_at(k):
        return sum(count_at(j) for j in range(k))

    def current(piece, p, k, a, bit):
        order, cols, part = piece[0], piece[1], piece[2]
        if k == 0:
            d = bit * (1 << order[0])
            for m in range(bits - 1):
                d = d + ((a >> m) & 1) * (1 << order[1 + m])
            return dw[p, d, :, cols]
        return part[offset_at(k - 1) + a * 2 + bit]

    def sum_copy(piece, p, k):
        _, _, _, send, land, ssem, rsem = piece
        at = pl.ds(offset_at(k), count_at(k))
        return pltpu.make_async_remote_copy(
            src_ref=send.at[at], dst_ref=land.at[at],
            send_sem=ssem.at[p, k], recv_sem=rsem.at[p, k],
            device_id=(partner(piece[0][k]), nbr), device_id_type=MESH,
        )

    def sum_send(p, k):
        for piece in pieces_of(p):
            bit = mine[piece[0][k]]
            for a in range(count_at(k)):
                piece[3][offset_at(k) + a] = current(piece, p, k, a, 1 - bit).astype(BF)
            sum_copy(piece, p, k).start()

    def sum_take(p, k):
        for piece in pieces_of(p):
            order, cols, part, _, land, _, _ = piece
            bit = mine[order[k]]
            sum_copy(piece, p, k).wait_recv()
            for a in range(count_at(k)):
                got = current(piece, p, k, a, bit) + land[offset_at(k) + a].astype(F32)
                if k < bits - 1:
                    part[offset_at(k) + a] = got
                else:
                    lo, hi = cols.start, cols.stop
                    for t, out in enumerate((gk_ref, gv_ref)):
                        a0, a1 = max(lo, t * PAIR), min(hi, (t + 1) * PAIR)
                        if a0 < a1:
                            base = p * PAIR - t * PAIR
                            out[:, base + a0 : base + a1] = got[:, a0 - lo : a1 - lo]

    def sum_step(p, k):
        sum_take(p, k)
        if k + 1 < bits:
            sum_send(p, k + 1)

    def collect(n):
        spread(n)[0].wait_recv()
        forward(n).start()

    def settle(n):
        spread(n)[1].wait_recv()
        forward(n).wait_recv()

    for h in range(halves):
        ns = [n for n in range(len(cuts)) if cuts[n][0] == h]
        for n in ns:
            collect(n)
        if h == 0:
            loads[2].wait()
            loads[3].wait()
        if h == halves - 1:
            start(qg_copies(1)[EARLY:])
            start(qg_copies(2)[:SECOND])
        for n in ns:
            settle(n)
        project(0, [h])
        transpose(h)
    for p in range(pairs):
        if p == 0:
            start(qg_copies(2)[SECOND:])
        if 0 < p < pairs - 2:
            start(qg_copies(p + 2))
        if p:
            project(p, range(halves))
        if p == 0 and not EARLY or p > 0:
            for c in qg_copies(p):
                c.wait_recv()
        for c in qg_local(p):
            c.wait()
        if p == HOLD:
            for before in range(p):
                start(att_copies(before))
        attend(p)
        if p >= HOLD:
            start(att_copies(p))
        att_local(p).start()
        weight_grads(p)
        sum_send(p, 0)
        for k in range(bits):
            if p - 1 - k >= 0:
                sum_step(p - 1 - k, k)
    for k in range(bits):
        for back in range(1, bits - k):
            sum_step(pairs - 1 - back, k + back)
        sum_step(pairs - 1, k)

    for p in range(pairs):
        for c in att_copies(p):
            c.wait_recv()
            c.wait_send()
        att_local(p).wait()
        for c in qg_copies(p):
            c.wait_send()
        for piece in pieces_of(p):
            for k in range(bits):
                sum_copy(piece, p, k).wait_send()
    for n in range(len(cuts)):
        for c in spread(n) + [forward(n)]:
            c.wait_send()
    for c in a2a_copies(len(cuts) - 1):
        c.wait_send()


EARLY = 3
SECOND = 0
HOLD = 3
CUTS = (256, 384, 384, 384)


def column_cuts(halves, width):
    middle = (width // HEAD + 1) // 2 * HEAD
    cuts = [(0, slice(0, width))]
    for h in range(1, halves):
        cuts += [(h, slice(0, middle)), (h, slice(middle, width))]
    return cuts


TILE_GROUPS = 4
TOGETHER = 3


def fused(queries, cotangent, pool, enc_gain, enc_weight, k_weight, v_weight, owner, slot):
    n_dp, n_nbr = lax.axis_size("dp"), lax.axis_size("nbr")
    held, tokens, width = pool.shape
    own_rows, model = queries.shape
    groups = owner.shape[0] // n_dp
    halves = tokens // ROWS
    pairs = k_weight.shape[1] // PAIR
    bits = n_dp.bit_length() - 1
    block = width // n_dp
    keys = groups * n_nbr * tokens
    steps = (1 << bits) - 1
    cuts = column_cuts(halves, width)
    wide = [cols.stop - cols.start for _, cols in cuts]
    rest = [max(2 * PAIR - cut, HEAD) for cut in CUTS]
    code = (owner * held + slot).reshape(-1)
    anywhere = pl.BlockSpec(memory_space=pl.ANY)
    vmem = pl.BlockSpec(memory_space=pltpu.VMEM)
    dma = pltpu.SemaphoreType.DMA
    out = pl.pallas_call(
        fused_body,
        in_specs=[pl.BlockSpec(memory_space=pltpu.SMEM), vmem] + [anywhere] * 6,
        out_specs=[vmem, vmem, vmem],
        out_shape=[
            pltpu.VMEM(queries.shape, BF),
            jax.ShapeDtypeStruct((block, k_weight.shape[1]), F32),
            jax.ShapeDtypeStruct((block, v_weight.shape[1]), F32),
        ],
        scratch_shapes=[
            pltpu.VMEM(pool.shape, BF),
            pltpu.VMEM(enc_weight.shape, BF),
            pltpu.VMEM((2,) + k_weight.shape, BF),
            pltpu.VMEM((halves, held, ROWS, width), BF),
            [pltpu.VMEM((n_dp, CAP, ROWS, w), BF) for w in wide],
            [pltpu.VMEM((n_dp * CAP, ROWS, w), BF) for w in wide],
            pltpu.VMEM((halves, groups, n_nbr, ROWS, width), BF),
            pltpu.VMEM((width, keys), BF),
            pltpu.VMEM((pairs, (groups + 1) * GROUP, PAIR), BF),
            pltpu.VMEM((pairs, (groups + 1) * GROUP, PAIR), BF),
            pltpu.VMEM((pairs, (groups + 1) * GROUP, PAIR), BF),
            pltpu.VMEM((2, keys, PAIR), BF),
            pltpu.VMEM((2, keys, PAIR), BF),
            pltpu.VMEM((pairs, n_dp, block, 2 * PAIR), F32),
            [pltpu.VMEM((steps, block, n), F32) for n in CUTS],
            [pltpu.VMEM((steps, block, n), BF) for n in CUTS],
            [pltpu.VMEM((steps, block, n), BF) for n in CUTS],
            [pltpu.VMEM((steps, block, n), F32) for n in rest],
            [pltpu.VMEM((steps, block, n), BF) for n in rest],
            [pltpu.VMEM((steps, block, n), BF) for n in rest],
            dma((4,)),
            dma((pairs, 2, 3)), dma((pairs, 2, 3)), dma((pairs, 2)),
            dma((len(cuts), n_dp - 1)), dma((len(cuts), n_dp - 1)),
            dma((len(cuts), 3)), dma((len(cuts), 3)),
            dma((pairs, 3)), dma((pairs, 3)), dma((pairs,)),
            dma((pairs, bits)), dma((pairs, bits)), dma((pairs, bits)), dma((pairs, bits)),
        ],
        compiler_params=pltpu.CompilerParams(
            collective_id=0, has_side_effects=True, vmem_limit_bytes=58 * 2**20
        ),
    )(code, enc_gain, queries, cotangent, pool, enc_weight, k_weight, v_weight)
    return tuple(out)


def per_device(
    queries, cotangent, pool, enc_gain, enc_weight, k_weight, v_weight, nbr_owner, nbr_slot
):
    n_dp, n_nbr = lax.axis_size("dp"), lax.axis_size("nbr")
    _, tokens, width = pool.shape
    groups = nbr_owner.shape[0] // n_dp
    args = (
        queries, cotangent, pool, enc_gain, enc_weight, k_weight, v_weight, nbr_owner, nbr_slot
    )
    fits = (
        n_nbr == 4
        and n_dp & (n_dp - 1) == 0
        and width % (n_dp * ROWS) == 0
        and tokens % ROWS == 0
        and tokens > ROWS
        and k_weight.shape[1] == PAIR * len(CUTS)
        and groups % TILE_GROUPS == 0
        and groups % TOGETHER == 0
        and HEAD % (n_nbr * ROWS) == 0
    )
    return fused(*args) if fits else staged(*args)


def solution(mesh):
    return jax.shard_map(
        per_device,
        mesh=mesh,
        in_specs=(
            P(("dp", "nbr"), None),
            P(("dp", "nbr"), None),
            P("dp", "nbr", None),
            P(),
            P(),
            P(None, "nbr"),
            P(None, "nbr"),
            P(),
            P(),
        ),
        out_specs=(P(("dp", "nbr"), None), P("dp", "nbr"), P("dp", "nbr")),
        check_vma=False,
    )
```

```python
import jax
import jax.numpy as jnp
from jax import lax
from jax.experimental import pallas as pl
from jax.experimental.pallas import tpu as pltpu
from jax.sharding import PartitionSpec as P

HEAD = 128
GROUP = 64
CAP = 2
BF = jnp.bfloat16
F32 = jnp.float32


def encode(blocks, gain_vec, weight):
    widened = blocks.astype(F32)
    mean_sq = jnp.mean(widened * widened, axis=-1, keepdims=True)
    normed = (widened * lax.rsqrt(mean_sq + 1e-06) * gain_vec).astype(BF)
    combined = jnp.dot(normed, weight, preferred_element_type=F32)
    return (widened + jax.nn.gelu(combined)).astype(BF)


def pick_rows(chosen, rows, tokens):
    m, n = chosen.shape
    eye = jnp.eye(tokens, dtype=BF)
    full = chosen.astype(BF)[:, None, :, None] * eye[None, :, None, :]
    full = full.reshape(m * tokens, n * tokens)
    return jnp.dot(full, rows, preferred_element_type=F32).astype(BF)


def attention_body(q_ref, g_ref, k_ref, v_ref, o_ref, dk_ref, dv_ref):
    heads = q_ref.shape[1] // HEAD
    parts, _, tokens, _ = k_ref.shape
    keys = parts * tokens
    scale = HEAD ** (-0.5)
    over_last = (((1,), (1,)), ((), ()))
    over_first = (((0,), (0,)), ((), ()))
    for first in range(0, heads, 4):
        held = []
        for h in range(first, min(first + 4, heads)):
            cols = slice(h * HEAD, (h + 1) * HEAD)
            k = k_ref[:, 0, :, cols].reshape(keys, HEAD)
            v = v_ref[:, 0, :, cols].reshape(keys, HEAD)
            s = lax.dot_general(q_ref[:, cols], k, over_last, preferred_element_type=F32)
            dw = lax.dot_general(g_ref[:, cols], v, over_last, preferred_element_type=F32)
            held.append((cols, v, s * scale, dw.astype(BF).astype(F32)))
        ready = []
        for cols, v, s, dw in held:
            e = jnp.exp(s - jnp.max(s, axis=-1, keepdims=True))
            p = e * (1.0 / jnp.sum(e, axis=-1, keepdims=True))
            ds = p * (dw - jnp.sum(dw * p, axis=-1, keepdims=True)) * scale
            ready.append((cols, v, p.astype(BF), ds.astype(BF)))
        for cols, v, w, ds in ready:
            q, g = q_ref[:, cols], g_ref[:, cols]
            o_ref[:, cols] = jnp.dot(w, v, preferred_element_type=F32).astype(BF)
            dk = lax.dot_general(ds, q, over_first, preferred_element_type=F32)
            dv = lax.dot_general(w, g, over_first, preferred_element_type=F32)
            dk_ref[:, 0, :, cols] = dk.astype(BF).reshape(parts, tokens, HEAD)
            dv_ref[:, 0, :, cols] = dv.astype(BF).reshape(parts, tokens, HEAD)


def attention(q, g, k, v):
    length, width = q.shape
    parts, groups, tokens, _ = k.shape
    row = pl.BlockSpec((GROUP, width), lambda c: (c, 0))
    block = pl.BlockSpec((parts, 1, tokens, width), lambda c: (0, c, 0, 0))
    work = 10 * length * parts * tokens * width
    return pl.pallas_call(
        attention_body,
        grid=(groups,),
        in_specs=[row, row, block, block],
        out_specs=[row, block, block],
        out_shape=[
            jax.ShapeDtypeStruct(q.shape, BF),
            jax.ShapeDtypeStruct(k.shape, BF),
            jax.ShapeDtypeStruct(v.shape, BF),
        ],
        compiler_params=pltpu.CompilerParams(vmem_limit_bytes=32 * 2**20),
        cost_estimate=pl.CostEstimate(
            flops=work,
            bytes_accessed=6 * length * width + 8 * k.size,
            transcendentals=length * parts * tokens * width // HEAD,
        ),
    )(q, g, k, v)


def exchange(x, axis, split, join):
    n = lax.axis_size(axis)
    me = lax.axis_index(axis)
    span = x.shape[split] // n
    step = x.shape[join]
    parts = []
    for d in range(n):
        piece = lax.dynamic_slice_in_dim(x, (me ^ d) * span, span, split)
        if d:
            piece = lax.ppermute(piece, axis, [(i, i ^ d) for i in range(n)])
        parts.append(piece)
    shape = list(parts[0].shape)
    shape[join] = n * step
    whole = jnp.zeros(shape, x.dtype)
    for d, piece in enumerate(parts):
        whole = lax.dynamic_update_slice_in_dim(whole, piece, (me ^ d) * step, join)
    return whole


def halving(total, axis, turn):
    n = lax.axis_size(axis)
    me = lax.axis_index(axis)
    count = n.bit_length() - 1
    bits = [(i + turn) % count for i in range(count)]
    rows, width = total.shape
    current = total.reshape((2,) * count + (rows // n, width))
    left = list(range(count - 1, -1, -1))
    for bit in bits:
        place = left.index(bit)
        left.pop(place)
        mine = (me >> bit) & 1
        away = lax.dynamic_index_in_dim(current, 1 - mine, place, keepdims=False)
        keep = lax.dynamic_index_in_dim(current, mine, place, keepdims=False)
        pairs = [(i, i ^ (1 << bit)) for i in range(n)]
        current = keep + lax.ppermute(away.astype(BF), axis, pairs).astype(F32)
    return current


def staged(
    queries, cotangent, pool, enc_gain, enc_weight, k_weight, v_weight, nbr_owner, nbr_slot
):
    dp_count = lax.axis_size("dp")
    nbr_count = lax.axis_size("nbr")
    me = lax.axis_index("dp")
    held, tokens, enc_width = pool.shape
    per_row = nbr_owner.shape[0] // dp_count

    owners = nbr_owner[:, 0].reshape(dp_count, per_row)
    slots = nbr_slot[:, 0].reshape(dp_count, per_row)
    same = owners[:, :, None] == owners[:, None, :]
    earlier = jnp.tril(jnp.ones((per_row, per_row), jnp.bool_), -1)
    rank = jnp.sum((same & earlier[None]).astype(jnp.int32), axis=-1)

    ranks = jnp.arange(CAP, dtype=jnp.int32)
    blocks = jnp.arange(held, dtype=jnp.int32)
    mine = (owners == me)[:, None, :] & (rank[:, None, :] == ranks[None, :, None])
    send = jnp.any(
        mine[:, :, None, :] & (slots[:, None, None, :] == blocks[None, None, :, None]), axis=-1
    ).reshape(dp_count * CAP, held)
    enc = encode(pool.reshape(held * tokens, enc_width), enc_gain, enc_weight)
    outgoing = pick_rows(send, enc, tokens)
    arrived = lax.all_to_all(outgoing, "dp", split_axis=0, concat_axis=0, tiled=True)

    q_rows = exchange(queries, "nbr", 1, 0)
    arrived, q_rows = lax.optimization_barrier((arrived, q_rows))

    place = lax.dynamic_slice_in_dim(owners * CAP + rank, me, 1, 0)[0]
    take = place[:, None] == jnp.arange(dp_count * CAP, dtype=jnp.int32)[None, :]
    picked = pick_rows(take, arrived, tokens)
    flat_enc = lax.all_gather(picked, "nbr", axis=0, tiled=True)

    g_rows = exchange(cotangent, "nbr", 1, 0)
    seq_len, width = q_rows.shape
    lead = GROUP - 1
    blank = jnp.zeros((lead, width), BF)
    q_rows = jnp.concatenate([q_rows[lead:], blank], axis=0)
    g_rows = jnp.concatenate([g_rows[lead:], blank], axis=0)

    shape4 = (nbr_count, per_row, tokens, width)
    keys = jnp.dot(flat_enc, k_weight, preferred_element_type=F32).astype(BF)
    values = jnp.dot(flat_enc, v_weight, preferred_element_type=F32).astype(BF)
    out, dk, dv = attention(q_rows, g_rows, keys.reshape(shape4), values.reshape(shape4))

    over_first = (((0,), (0,)), ((), ()))

    def weight_grad(grads):
        return lax.dot_general(
            flat_enc, grads.reshape(-1, width), over_first, preferred_element_type=F32
        )

    grad_v = halving(weight_grad(dv), "dp", 0)
    product_k = weight_grad(dk)
    cut = width // HEAD * 3 // 8 * HEAD
    grad_k = jnp.concatenate(
        [halving(product_k[:, :cut], "dp", 0), halving(product_k[:, cut:], "dp", 1)], axis=1
    )
    out = jnp.concatenate([blank, out[: seq_len - lead]], axis=0)
    merged = exchange(out, "nbr", 0, 1)
    return (merged, grad_k, grad_v)


MESH = pl.DeviceIdType.MESH
ROWS = 16
PAIR = 2 * HEAD
LAST = (((1,), (1,)), ((), ()))
FIRST = (((0,), (0,)), ((), ()))


def gelu(x):
    return jax.nn.gelu(x)


def fused_body(
    code_ref, gain_ref, q_hbm, g_hbm, pool_hbm, encw_hbm, wk_hbm, wv_hbm,
    att_hbm, gk_ref, gv_ref,
    pool_v, encw_v, w_v, local, outboxes, inboxes, enc, enc_t, qs, gs, os,
    kv, dkv, dw, parts_a, sends_a, lands_a, parts_b, sends_b, lands_b,
    load_sem, qg_send, qg_recv, qg_own, a2a_send, a2a_recv, gat_send, gat_recv,
    att_send, att_recv, att_own, ra_send, ra_recv, rb_send, rb_recv,
):
    n_dp, n_nbr = lax.axis_size("dp"), lax.axis_size("nbr")
    dp, nbr = lax.axis_index("dp"), lax.axis_index("nbr")
    held, tokens, width = pool_v.shape
    halves, groups = enc.shape[:2]
    cuts = column_cuts(halves, width)
    pairs, _, _ = qs.shape
    own_rows = q_hbm.shape[0]
    keys = groups * n_nbr * ROWS
    per_group = n_nbr * ROWS
    bits = n_dp.bit_length() - 1

    chip, core = nbr // 2, nbr % 2
    mate = chip * 2 + (1 - core)
    across = ((chip + 1) * 2) % n_nbr + core
    diagonal = ((chip + 1) * 2) % n_nbr + (1 - core)
    nbr_peers = (across, diagonal, mate)
    dp_peers = [(dp + k) % n_dp for k in range(1, n_dp)]

    loads = [
        pltpu.make_async_copy(pool_hbm, pool_v, load_sem.at[0]),
        pltpu.make_async_copy(encw_hbm, encw_v, load_sem.at[1]),
        pltpu.make_async_copy(wk_hbm, w_v.at[0], load_sem.at[2]),
        pltpu.make_async_copy(wv_hbm, w_v.at[1], load_sem.at[3]),
    ]
    loads[0].start()
    loads[1].start()

    barrier = pltpu.get_barrier_semaphore()
    for peer in nbr_peers:
        pl.semaphore_signal(barrier, inc=1, device_id=(dp, peer), device_id_type=MESH)
    for peer in dp_peers:
        pl.semaphore_signal(barrier, inc=1, device_id=(peer, nbr), device_id_type=MESH)
    own_at = pl.ds(pl.multiple_of(nbr * own_rows, own_rows), own_rows)

    def head_cols(peer, p):
        return pl.ds(pl.multiple_of((peer * pairs + p) * PAIR, PAIR), PAIR)

    def qg_copies(p):
        made = []
        for t, (src, dst) in enumerate(((q_hbm, qs), (g_hbm, gs))):
            for k, peer in enumerate(nbr_peers):
                made.append(
                    pltpu.make_async_remote_copy(
                        src_ref=src.at[:, head_cols(peer, p)],
                        dst_ref=dst.at[p, own_at, :],
                        send_sem=qg_send.at[p, t, k],
                        recv_sem=qg_recv.at[p, t, k],
                        device_id=(dp, peer),
                        device_id_type=MESH,
                    )
                )
        return made

    def qg_local(p):
        return [
            pltpu.make_async_copy(
                src.at[:, head_cols(nbr, p)], dst.at[p, own_at, :], qg_own.at[p, t]
            )
            for t, (src, dst) in enumerate(((q_hbm, qs), (g_hbm, gs)))
        ]

    def start(copies):
        for c in copies:
            c.start()

    me = dp

    def chosen_for(s):
        count = jnp.int32(0)
        picks = [jnp.int32(0)] * CAP
        for u in range(groups):
            code = code_ref[s * groups + u]
            hit = code // held == me
            for r in range(CAP):
                picks[r] = jnp.where(hit & (count == r), code % held, picks[r])
            count = count + jnp.where(hit, 1, 0)
        return picks

    chosen = [chosen_for(s) for s in range(n_dp)]
    owners = [code_ref[me * groups + u] // held for u in range(groups)]
    places = []
    for u in range(groups):
        rank = jnp.int32(0)
        for w in range(u):
            rank = rank + jnp.where(owners[w] == owners[u], 1, 0)
        places.append(owners[u] * CAP + rank)

    def a2a_copies(n):
        return [
            pltpu.make_async_remote_copy(
                src_ref=outboxes[n].at[peer],
                dst_ref=inboxes[n].at[pl.ds(pl.multiple_of(me * CAP, CAP), CAP)],
                send_sem=a2a_send.at[n, k],
                recv_sem=a2a_recv.at[n, k],
                device_id=(peer, nbr),
                device_id_type=MESH,
            )
            for k, peer in enumerate(dp_peers)
        ]

    def encoded(x):
        x = x.astype(F32)
        mean_sq = jnp.mean(x * x, axis=-1, keepdims=True)
        normed = (x * lax.rsqrt(mean_sq + 1e-06) * gain_ref[...].reshape(1, width)).astype(BF)
        combined = jnp.dot(normed, encw_v[...], preferred_element_type=F32)
        return (x + jax.nn.gelu(combined)).astype(BF)

    def fill_outbox(n, block_at):
        for s in range(n_dp):
            for r in range(CAP):
                outboxes[n][s, r] = block_at(chosen[s][r])

    def keep_own(n):
        for r in range(CAP):
            inboxes[n][me * CAP + r] = outboxes[n][me, r]

    loads[0].wait()
    loads[1].wait()
    for h in range(halves):
        x = pool_v[:, h * ROWS : (h + 1) * ROWS, :].reshape(held * ROWS, width)
        local[h] = encoded(x).reshape(held, ROWS, width)
    for n, (h, cols) in enumerate(cuts):
        fill_outbox(n, lambda b: local[h, b, :, cols])
        keep_own(n)
    pl.semaphore_wait(barrier, len(nbr_peers) + len(dp_peers))
    start(a2a_copies(0))
    start(qg_copies(0))
    loads[2].start()
    loads[3].start()
    for p in range(pairs):
        start(qg_local(p))

    tail = jnp.zeros((GROUP, PAIR), BF)
    for p in range(pairs):
        qs[p, groups * GROUP : (groups + 1) * GROUP, :] = tail
        gs[p, groups * GROUP : (groups + 1) * GROUP, :] = tail
        os[p, 0:GROUP, :] = tail

    def spread(n):
        h, cols = cuts[n]
        part = enc.at[h, :, nbr, :, cols]
        return [
            pltpu.make_async_remote_copy(
                src_ref=part, dst_ref=part,
                send_sem=gat_send.at[n, k], recv_sem=gat_recv.at[n, k],
                device_id=(dp, peer), device_id_type=MESH,
            )
            for k, peer in enumerate((across, mate))
        ]

    def forward(n):
        h, cols = cuts[n]
        part = enc.at[h, :, across, :, cols]
        return pltpu.make_async_remote_copy(
            src_ref=part, dst_ref=part,
            send_sem=gat_send.at[n, 2], recv_sem=gat_recv.at[n, 2],
            device_id=(dp, mate), device_id_type=MESH,
        )

    def transpose(h):
        step = HEAD // per_group
        for u in range(0, groups, step):
            at = h * groups * per_group + u * per_group
            block = enc[h, u : u + step].reshape(HEAD, width)
            enc_t[:, at : at + HEAD] = block.T

    if EARLY:
        for c in qg_copies(0):
            c.wait_recv()
        start(qg_copies(1)[:EARLY])
    for n, (h, cols) in enumerate(cuts):
        if n + 1 < len(cuts):
            for c in a2a_copies(n):
                c.wait_send()
            start(a2a_copies(n + 1))
        for c in a2a_copies(n):
            c.wait_recv()
        for u in range(groups):
            enc[h, u, nbr, :, cols] = inboxes[n][places[u]]
        start(spread(n))

    def project(p, hs):
        cols = slice(p * PAIR, (p + 1) * PAIR)
        for h in hs:
            def tile(i, _):
                u = i * TILE_GROUPS
                rows = TILE_GROUPS * per_group
                e = enc[h, pl.ds(u, TILE_GROUPS)].reshape(rows, width)
                at = pl.ds(pl.multiple_of(h * groups * per_group + u * per_group, rows), rows)
                for t in range(2):
                    kv[t, at, :] = jnp.dot(
                        e, w_v[t, :, cols], preferred_element_type=F32
                    ).astype(BF)
                return 0
            lax.fori_loop(0, groups // TILE_GROUPS, tile, 0)

    scale = HEAD ** (-0.5)
    last_row = lax.broadcasted_iota(jnp.int32, (ROWS, PAIR), 0) == ROWS - 1
    blank = jnp.zeros((GROUP, HEAD), BF)

    def rows_of(ref, p, u):
        here = ref[p, pl.ds(pl.multiple_of(u * GROUP + GROUP - ROWS, ROWS), ROWS), :]
        after = ref[p, pl.ds(pl.multiple_of((u + 1) * GROUP, GROUP), GROUP), :]
        end = jnp.where(last_row, here, after[GROUP - ROWS :])
        got = jnp.concatenate([after[: GROUP - ROWS], end], axis=0)
        return jnp.concatenate(
            [
                jnp.concatenate([got[:, :HEAD], blank], axis=1),
                jnp.concatenate([blank, got[:, HEAD:]], axis=1),
            ],
            axis=0,
        )

    def key_rows(u):
        return [
            pl.ds(pl.multiple_of(h * groups * per_group + u * per_group, per_group), per_group)
            for h in range(halves)
        ]

    def attend(p):
        def several(i, _):
            us = [i * TOGETHER + j for j in range(TOGETHER)]
            held_now = []
            for u in us:
                at = key_rows(u)
                k = jnp.concatenate([kv[0, a, :] for a in at], axis=0)
                v = jnp.concatenate([kv[1, a, :] for a in at], axis=0)
                q, g = rows_of(qs, p, u), rows_of(gs, p, u)
                s = lax.dot_general(k, q, LAST, preferred_element_type=F32) * scale
                d = lax.dot_general(v, g, LAST, preferred_element_type=F32)
                held_now.append((v, q, g, s, d.astype(BF).astype(F32)))
            ready = []
            for v, q, g, s, d in held_now:
                e = jnp.exp(s - jnp.max(s, axis=0, keepdims=True))
                w = e * (1.0 / jnp.sum(e, axis=0, keepdims=True))
                ds = w * (d - jnp.sum(d * w, axis=0, keepdims=True)) * scale
                ready.append((v, q, g, w.astype(BF), ds.astype(BF)))
            for u, (v, q, g, w, ds) in zip(us, ready):
                o = lax.dot_general(w, v, FIRST, preferred_element_type=F32)
                o = jnp.concatenate([o[:GROUP, :HEAD], o[GROUP:, HEAD:]], axis=1).astype(BF)
                dk = jnp.dot(ds, q, preferred_element_type=F32).astype(BF)
                dv = jnp.dot(w, g, preferred_element_type=F32).astype(BF)
                for h, a in enumerate(key_rows(u)):
                    dkv[0, a, :] = dk[h * per_group : (h + 1) * per_group]
                    dkv[1, a, :] = dv[h * per_group : (h + 1) * per_group]
                end = pl.ds(pl.multiple_of(u * GROUP + GROUP - ROWS, ROWS), ROWS)
                os[p, end, :] = jnp.where(last_row, o[GROUP - ROWS :], os[p, end, :])
                os[p, pl.ds(pl.multiple_of((u + 1) * GROUP, GROUP), GROUP), :] = o
            return 0
        lax.fori_loop(0, groups // TOGETHER, several, 0)

    def att_copies(p):
        return [
            pltpu.make_async_remote_copy(
                src_ref=os.at[p, pl.ds(pl.multiple_of(peer * own_rows, own_rows), own_rows), :],
                dst_ref=att_hbm.at[:, head_cols(nbr, p)],
                send_sem=att_send.at[p, k], recv_sem=att_recv.at[p, k],
                device_id=(dp, peer), device_id_type=MESH,
            )
            for k, peer in enumerate(nbr_peers)
        ]

    def att_local(p):
        return pltpu.make_async_copy(
            os.at[p, own_at, :], att_hbm.at[:, head_cols(nbr, p)], att_own.at[p]
        )

    def weight_grads(p):
        for t in range(2):
            got = jnp.dot(enc_t[...], dkv[t], preferred_element_type=F32)
            dw[p, :, :, t * PAIR : (t + 1) * PAIR] = got.reshape(n_dp, width // n_dp, PAIR)

    mine = [(me // (1 << b)) % 2 for b in range(bits)]

    def partner(b):
        return me + (1 - 2 * mine[b]) * (1 << b)

    def pieces_of(p):
        made = []
        orders = (tuple(range(bits)), tuple(range(1, bits)) + (0,))
        stacks = ((parts_a, sends_a, lands_a), (parts_b, sends_b, lands_b))
        for n, (lo, hi) in enumerate(((0, CUTS[p]), (CUTS[p], 2 * PAIR))):
            if lo < hi:
                part, send, land = (x[p] for x in stacks[n])
                sems = (ra_send, ra_recv) if n == 0 else (rb_send, rb_recv)
                made.append((orders[n], slice(lo, hi), part, send, land) + sems)
        return made

    def count_at(k):
        return 1 << (bits - 1 - k)

    def offset_at(k):
        return sum(count_at(j) for j in range(k))

    def current(piece, p, k, a, bit):
        order, cols, part = piece[0], piece[1], piece[2]
        if k == 0:
            d = bit * (1 << order[0])
            for m in range(bits - 1):
                d = d + ((a >> m) & 1) * (1 << order[1 + m])
            return dw[p, d, :, cols]
        return part[offset_at(k - 1) + a * 2 + bit]

    def sum_copy(piece, p, k):
        _, _, _, send, land, ssem, rsem = piece
        at = pl.ds(offset_at(k), count_at(k))
        return pltpu.make_async_remote_copy(
            src_ref=send.at[at], dst_ref=land.at[at],
            send_sem=ssem.at[p, k], recv_sem=rsem.at[p, k],
            device_id=(partner(piece[0][k]), nbr), device_id_type=MESH,
        )

    def sum_send(p, k):
        for piece in pieces_of(p):
            bit = mine[piece[0][k]]
            for a in range(count_at(k)):
                piece[3][offset_at(k) + a] = current(piece, p, k, a, 1 - bit).astype(BF)
            sum_copy(piece, p, k).start()

    def sum_take(p, k):
        for piece in pieces_of(p):
            order, cols, part, _, land, _, _ = piece
            bit = mine[order[k]]
            sum_copy(piece, p, k).wait_recv()
            for a in range(count_at(k)):
                got = current(piece, p, k, a, bit) + land[offset_at(k) + a].astype(F32)
                if k < bits - 1:
                    part[offset_at(k) + a] = got
                else:
                    lo, hi = cols.start, cols.stop
                    for t, out in enumerate((gk_ref, gv_ref)):
                        a0, a1 = max(lo, t * PAIR), min(hi, (t + 1) * PAIR)
                        if a0 < a1:
                            base = p * PAIR - t * PAIR
                            out[:, base + a0 : base + a1] = got[:, a0 - lo : a1 - lo]

    def sum_step(p, k):
        sum_take(p, k)
        if k + 1 < bits:
            sum_send(p, k + 1)

    def collect(n):
        spread(n)[0].wait_recv()
        forward(n).start()

    def settle(n):
        spread(n)[1].wait_recv()
        forward(n).wait_recv()

    for h in range(halves):
        ns = [n for n in range(len(cuts)) if cuts[n][0] == h]
        for n in ns:
            collect(n)
        if h == 0:
            loads[2].wait()
            loads[3].wait()
        if h == halves - 1:
            start(qg_copies(1)[EARLY:])
            start(qg_copies(2)[:SECOND])
        for n in ns:
            settle(n)
        project(0, [h])
        transpose(h)
    for p in range(pairs):
        if p == 0:
            start(qg_copies(2)[SECOND:])
        if 0 < p < pairs - 2:
            start(qg_copies(p + 2))
        if p:
            project(p, range(halves))
        if p == 0 and not EARLY or p > 0:
            for c in qg_copies(p):
                c.wait_recv()
        for c in qg_local(p):
            c.wait()
        if p == HOLD:
            for before in range(p):
                start(att_copies(before))
        attend(p)
        if p >= HOLD:
            start(att_copies(p))
        att_local(p).start()
        weight_grads(p)
        sum_send(p, 0)
        for k in range(bits):
            if p - 1 - k >= 0:
                sum_step(p - 1 - k, k)
    for k in range(bits):
        for back in range(1, bits - k):
            sum_step(pairs - 1 - back, k + back)
        sum_step(pairs - 1, k)

    for p in range(pairs):
        for c in att_copies(p):
            c.wait_recv()
            c.wait_send()
        att_local(p).wait()
        for c in qg_copies(p):
            c.wait_send()
        for piece in pieces_of(p):
            for k in range(bits):
                sum_copy(piece, p, k).wait_send()
    for n in range(len(cuts)):
        for c in spread(n) + [forward(n)]:
            c.wait_send()
    for c in a2a_copies(len(cuts) - 1):
        c.wait_send()


EARLY = 3
SECOND = 0
HOLD = 3
CUTS = (256, 384, 384, 384)


def column_cuts(halves, width):
    middle = (width // HEAD + 1) // 2 * HEAD
    cuts = [(0, slice(0, width))]
    for h in range(1, halves):
        cuts += [(h, slice(0, middle)), (h, slice(middle, width))]
    return cuts


TILE_GROUPS = 4
TOGETHER = 3


def fused(queries, cotangent, pool, enc_gain, enc_weight, k_weight, v_weight, owner, slot):
    n_dp, n_nbr = lax.axis_size("dp"), lax.axis_size("nbr")
    held, tokens, width = pool.shape
    own_rows, model = queries.shape
    groups = owner.shape[0] // n_dp
    halves = tokens // ROWS
    pairs = k_weight.shape[1] // PAIR
    bits = n_dp.bit_length() - 1
    block = width // n_dp
    keys = groups * n_nbr * tokens
    steps = (1 << bits) - 1
    cuts = column_cuts(halves, width)
    wide = [cols.stop - cols.start for _, cols in cuts]
    rest = [max(2 * PAIR - cut, HEAD) for cut in CUTS]
    code = (owner * held + slot).reshape(-1)
    anywhere = pl.BlockSpec(memory_space=pl.ANY)
    vmem = pl.BlockSpec(memory_space=pltpu.VMEM)
    dma = pltpu.SemaphoreType.DMA
    out = pl.pallas_call(
        fused_body,
        in_specs=[pl.BlockSpec(memory_space=pltpu.SMEM), vmem] + [anywhere] * 6,
        out_specs=[vmem, vmem, vmem],
        out_shape=[
            pltpu.VMEM(queries.shape, BF),
            pltpu.VMEM((block, k_weight.shape[1]), F32),
            pltpu.VMEM((block, v_weight.shape[1]), F32),
        ],
        scratch_shapes=[
            pltpu.VMEM(pool.shape, BF),
            pltpu.VMEM(enc_weight.shape, BF),
            pltpu.VMEM((2,) + k_weight.shape, BF),
            pltpu.VMEM((halves, held, ROWS, width), BF),
            [pltpu.VMEM((n_dp, CAP, ROWS, w), BF) for w in wide],
            [pltpu.VMEM((n_dp * CAP, ROWS, w), BF) for w in wide],
            pltpu.VMEM((halves, groups, n_nbr, ROWS, width), BF),
            pltpu.VMEM((width, keys), BF),
            pltpu.VMEM((pairs, (groups + 1) * GROUP, PAIR), BF),
            pltpu.VMEM((pairs, (groups + 1) * GROUP, PAIR), BF),
            pltpu.VMEM((pairs, (groups + 1) * GROUP, PAIR), BF),
            pltpu.VMEM((2, keys, PAIR), BF),
            pltpu.VMEM((2, keys, PAIR), BF),
            pltpu.VMEM((pairs, n_dp, block, 2 * PAIR), F32),
            [pltpu.VMEM((steps, block, n), F32) for n in CUTS],
            [pltpu.VMEM((steps, block, n), BF) for n in CUTS],
            [pltpu.VMEM((steps, block, n), BF) for n in CUTS],
            [pltpu.VMEM((steps, block, n), F32) for n in rest],
            [pltpu.VMEM((steps, block, n), BF) for n in rest],
            [pltpu.VMEM((steps, block, n), BF) for n in rest],
            dma((4,)),
            dma((pairs, 2, 3)), dma((pairs, 2, 3)), dma((pairs, 2)),
            dma((len(cuts), n_dp - 1)), dma((len(cuts), n_dp - 1)),
            dma((len(cuts), 3)), dma((len(cuts), 3)),
            dma((pairs, 3)), dma((pairs, 3)), dma((pairs,)),
            dma((pairs, bits)), dma((pairs, bits)), dma((pairs, bits)), dma((pairs, bits)),
        ],
        compiler_params=pltpu.CompilerParams(
            collective_id=0, has_side_effects=True, vmem_limit_bytes=58 * 2**20
        ),
    )(code, enc_gain, queries, cotangent, pool, enc_weight, k_weight, v_weight)
    return tuple(out)


def per_device(
    queries, cotangent, pool, enc_gain, enc_weight, k_weight, v_weight, nbr_owner, nbr_slot
):
    n_dp, n_nbr = lax.axis_size("dp"), lax.axis_size("nbr")
    _, tokens, width = pool.shape
    groups = nbr_owner.shape[0] // n_dp
    args = (
        queries, cotangent, pool, enc_gain, enc_weight, k_weight, v_weight, nbr_owner, nbr_slot
    )
    fits = (
        n_nbr == 4
        and n_dp & (n_dp - 1) == 0
        and width % (n_dp * ROWS) == 0
        and tokens % ROWS == 0
        and tokens > ROWS
        and k_weight.shape[1] == PAIR * len(CUTS)
        and groups % TILE_GROUPS == 0
        and groups % TOGETHER == 0
        and HEAD % (n_nbr * ROWS) == 0
    )
    return fused(*args) if fits else staged(*args)


def solution(mesh):
    return jax.shard_map(
        per_device,
        mesh=mesh,
        in_specs=(
            P(("dp", "nbr"), None),
            P(("dp", "nbr"), None),
            P("dp", "nbr", None),
            P(),
            P(),
            P(None, "nbr"),
            P(None, "nbr"),
            P(),
            P(),
        ),
        out_specs=(P(("dp", "nbr"), None), P("dp", "nbr"), P("dp", "nbr")),
        check_vma=False,
    )
```
